256 devices in a mesh: dom: 32 (over z, x), col: 8 (over y, core).
Axes of the slice: x: 4, y: 4, z: 8, core: 2. Of those that a mesh axis runs over, the one named last changes fastest.
Arguments:
- features: bfloat16 [65536, 128], P(('dom', 'col'))
- w_hidden: bfloat16 [128, 256], replicated, may hold values from -0.5 to 0.5
- w_out: bfloat16 [256, 256], replicated, may hold values from -0.375 to 0.375
- block_values: bfloat16 [8192, 4096], P('dom'), may hold values from 0.0009994507 to 1
- block_slot: int32 [8192], P('dom'), may hold values from 0 to 159, as said below
- requested: int32 [32, 32, 4], P('dom'), may hold values from -1 to 31, as said below
- labels: int32 [65536], P('dom'), may hold values from 0 to 171
- train_mask: int32 [65536], P('dom'), may hold values 0 or 1
Outputs:
- propagated: float32 [256, 65536], P('col', 'dom')
- logit_grad: float32 [256, 65536], P('col', 'dom')
The draws below stay inside these ranges and needn't reach their ends.
Inputs may be any that keep to these rules, and one draw needn't show every extreme that they name: requested[q, p, :] lists distinct row blocks of partition p first and -1 for the rest; it is all -1 for p = q and has at least one entry for every other p; for each q some p has all 4 entries. `block_slot`: each slot s >= 32 that a block of partition q names has requested[q, (s - 32) // 4, (s - 32) % 4] >= 0, and every such entry of requested is named by exactly one block of q; partition 0 reads 4 blocks from the last partition.
All inputs are finite; a program needn't handle non-finite values. No bound on the sum of `train_mask` on one device may be relied on, other than what follows from the above.
Results may differ from the reference program's by a relative error of at most 0.0037.
Values may be sent and summed in bfloat16 or wider, within the bound.
A program may use at most 64 MiB of HBM per device.

```python
import math
import jax
import jax.numpy as jnp
from jax import lax

FEAT = 128
HID = 256
LOGITS = 256
NCLASS = 172
BLOCK = 64
RB = 32
BPR = 8
CAP = 4
STEPS = 3
DOMAINS = 32
NODES = 65536
NBLK = 8192


def draw_features(key, part):
    key_noise, key_scale = jax.random.split(key, 2)
    noise = jax.random.normal(key_noise, (NODES, FEAT), jnp.float32)
    noise = jnp.clip(noise, -5.0, 5.0)
    row_scale = jnp.exp(jax.random.uniform(key_scale, (NODES, 1), jnp.float32) * jnp.log(10.0))
    return (noise * row_scale).astype(jnp.bfloat16)


def layout(key):
    folded = jax.random.fold_in(key, 31)
    key_count, key_peer, key_pick, key_local, key_order = jax.random.split(folded, 5)
    part_ids = jnp.arange(DOMAINS, dtype=jnp.int32)
    counts = jax.random.randint(key_count, (DOMAINS, DOMAINS), 1, CAP + 1)
    offset = jax.random.randint(key_peer, (DOMAINS,), 1, max(DOMAINS, 2))
    hub_peer = (part_ids + offset) % DOMAINS
    counts = jnp.where(part_ids[None, :] == hub_peer[:, None], CAP, counts)
    counts = counts.at[0, DOMAINS - 1].set(CAP)
    counts = jnp.where(part_ids[None, :] == part_ids[:, None], 0, counts)
    pair_keys = jax.random.split(key_pick, DOMAINS * DOMAINS)
    chosen = jax.vmap(lambda k: jax.random.permutation(k, RB)[:CAP])(pair_keys).reshape(DOMAINS, DOMAINS, CAP)
    lane_ids = jnp.arange(CAP, dtype=jnp.int32)
    wanted = jnp.where(lane_ids[None, None, :] < counts[:, :, None], chosen, -1).astype(jnp.int32)
    entries = RB * BPR
    local_rows = jax.random.randint(key_local, (DOMAINS, entries), 0, RB).astype(jnp.int32)
    usable = (wanted >= 0).reshape(DOMAINS, DOMAINS * CAP)
    remote_ids = RB + jnp.arange(DOMAINS * CAP, dtype=jnp.int32)
    order_keys = jax.random.split(key_order, DOMAINS)

    def place_slots(k, row_slots, usable_row):
        positions = jax.random.permutation(k, entries)[:DOMAINS * CAP]
        return row_slots.at[positions].set(jnp.where(usable_row, remote_ids, row_slots[positions]))
    slot_ids = jax.vmap(place_slots)(order_keys, local_rows, usable)
    return (wanted, slot_ids.reshape(-1).astype(jnp.int32))


def draw_requested(key, part):
    wanted, slot_ids = layout(key)
    return wanted


def draw_block_slot(key, part):
    wanted, slot_ids = layout(key)
    return slot_ids


def set_ends(drawn, own_key, smallest, top_value):
    extent = drawn.shape
    place = [jax.random.randint(jax.random.fold_in(own_key, axis), (), 0, extent[axis]) for axis in range(len(extent))]
    drawn = drawn.at[tuple(place)].set(smallest)
    longest = extent.index(max(extent))
    place[longest] = (place[longest] + 1) % extent[longest]
    return drawn.at[tuple(place)].set(top_value)


def block_levels(key, dims, shards, least, high):
    level, own = 1.0, jax.random.fold_in(key, 6)
    for position, blocks in shards:
        steps = jnp.exp(jax.random.uniform(jax.random.fold_in(own, position), (blocks,), jnp.float32, least / len(shards), high / len(shards)))
        level = level * jnp.repeat(steps, dims[position] // blocks).reshape([-1 if axis == position else 1 for axis in range(len(dims))])
    return level


def centred(rng, extent, spread, limit, held_as=jnp.bfloat16):
    values = jax.random.normal(rng, extent, jnp.float32) * spread
    return jnp.minimum(jnp.maximum(values, -limit), limit).astype(held_as)


def setup_inputs(seed: int = 0) -> dict:
    arg_keys = jax.random.split(jax.random.key(seed), 9)
    features = draw_features(jax.random.fold_in(arg_keys[8], 71), 0)
    w_hidden = centred(arg_keys[1], (FEAT, HID), FEAT ** -0.5, 0.5)
    w_out = centred(arg_keys[2], (HID, LOGITS), HID ** -0.5, 0.375)
    block_values = jnp.clip(jnp.exp(math.log(1.0) - 6.9083047 * jax.random.uniform(arg_keys[3], (NBLK, BLOCK * BLOCK), jnp.float32) ** block_levels(arg_keys[3], (NBLK, BLOCK * BLOCK), ((0, 32),), -0.2, 0.2)), 0.0009994507, 1.0).astype(jnp.bfloat16)
    block_slot = draw_block_slot(jax.random.fold_in(arg_keys[8], 71), 0)
    requested = draw_requested(jax.random.fold_in(arg_keys[8], 71), 0)
    labels = set_ends(jax.random.randint(arg_keys[6], (NODES,), 0, NCLASS), jax.random.fold_in(arg_keys[6], 1), 0, NCLASS - 1).astype(jnp.int32)
    train_mask = set_ends((jax.random.randint(arg_keys[7], (NODES,), 0, 2) < 1).astype(jnp.int32), jax.random.fold_in(arg_keys[7], 1), 0, 1)
    return {"features": features, "w_hidden": w_hidden, "w_out": w_out, "block_values": block_values, "block_slot": block_slot, "requested": requested, "labels": labels, "train_mask": train_mask}


TELEPORT = 0.1
masked_fill = -1e30


def reference(features, w_hidden, w_out, block_values, block_slot, requested, labels, train_mask):
    block_count = NODES // BLOCK
    hidden = jax.nn.relu(jnp.dot(features, w_hidden, preferred_element_type=jnp.float32)).astype(jnp.bfloat16)
    heads = jnp.dot(hidden, w_out, preferred_element_type=jnp.float32).astype(jnp.bfloat16)
    teleport = heads.reshape(block_count, BLOCK, LOGITS).transpose(0, 2, 1).astype(jnp.float32)
    tile_values = block_values.reshape(DOMAINS, RB * BPR, BLOCK, BLOCK)
    degree = jnp.sum(tile_values, axis=3, dtype=jnp.float32).reshape(DOMAINS, RB, BPR, BLOCK).sum(axis=2)
    inverse = (1.0 / (1.0 + degree)).reshape(block_count, 1, BLOCK)
    slot_ids = block_slot.reshape(DOMAINS, RB * BPR)
    part_ids = jnp.arange(DOMAINS, dtype=jnp.int32)[:, None]
    remote = jnp.maximum(slot_ids - RB, 0)
    peer = remote // CAP
    lane = remote % CAP
    chosen = requested[part_ids, peer, lane]
    global_cols = jnp.where(slot_ids < RB, part_ids * RB + slot_ids, peer * RB + chosen).astype(jnp.int32)
    parts = jnp.arange(DOMAINS, dtype=jnp.int32)

    def propagate(current):
        rounded = current.astype(jnp.bfloat16)

        def per_part(q):
            blocks = rounded[global_cols[q]].astype(jnp.float32)
            tiles = tile_values[q].astype(jnp.float32)
            products = jnp.einsum('ecj,eij->eci', blocks, tiles)
            return products.reshape(RB, BPR, LOGITS, BLOCK).sum(axis=1)

        summed = lax.map(per_part, parts).reshape(block_count, LOGITS, BLOCK)
        return (1.0 - TELEPORT) * ((summed + rounded.astype(jnp.float32)) * inverse) + TELEPORT * teleport

    def transpose_step(cotangent):
        scaled = (inverse * cotangent).astype(jnp.bfloat16)

        def per_part(totals, q):
            rows_part = lax.dynamic_slice_in_dim(scaled, q * RB, RB, 0).astype(jnp.float32)
            tiles = tile_values[q].reshape(RB, BPR, BLOCK, BLOCK).astype(jnp.float32)
            contrib = jnp.einsum('rci,rbij->rbcj', rows_part, tiles).reshape(RB * BPR, LOGITS, BLOCK)
            return totals.at[global_cols[q]].add(contrib), None

        totals, unused = lax.scan(per_part, jnp.zeros((block_count, LOGITS, BLOCK), jnp.float32), parts)
        return (1.0 - TELEPORT) * (totals + scaled.astype(jnp.float32))

    current = teleport
    for layer_step in range(STEPS):
        current = propagate(current)
    class_ids = jnp.arange(LOGITS, dtype=jnp.int32)[None, :, None]
    usable = class_ids < NCLASS
    row_max = jnp.max(jnp.where(usable, current, masked_fill), axis=1, keepdims=True)
    expo = jnp.where(usable, jnp.exp(current - row_max), 0.0)
    probs = expo / jnp.sum(expo, axis=1, keepdims=True)
    label_rows = labels.reshape(block_count, 1, BLOCK)
    onehot = (class_ids == label_rows).astype(jnp.float32)
    weight = train_mask.reshape(block_count, 1, BLOCK).astype(jnp.float32)
    cotangent = jnp.where(usable, weight * (probs - onehot), 0.0)
    gradient = TELEPORT * cotangent
    for layer_step in range(STEPS - 1, -1, -1):
        cotangent = transpose_step(cotangent)
        if layer_step > 0:
            gradient = gradient + TELEPORT * cotangent
        else:
            gradient = gradient + cotangent
    propagated = current.transpose(1, 0, 2).reshape(LOGITS, NODES)
    logit_grad = gradient.transpose(1, 0, 2).reshape(LOGITS, NODES)
    return (propagated, logit_grad)
```

```python
import functools

import jax
import jax.numpy as jnp
from jax import lax
from jax.experimental import pallas as pl
from jax.experimental.pallas import tpu as pltpu
from jax.sharding import PartitionSpec as P

NCLASS = 172
BLOCK = 64
STEPS = 3
CAP = 4
TELEPORT = 0.1
FILL = -1e30

HALF = 16
LANES = 128
PEER = CAP * HALF

F32 = jnp.float32
BF16 = jnp.bfloat16


def index_tables(block_slot, doms, row_blocks):
    entries = block_slot.shape[0]
    me = lax.axis_index("dom")
    chunks = (entries - (doms - 1) + row_blocks) // 2
    entry = jnp.arange(entries, dtype=jnp.int32)
    blocks = jnp.arange(row_blocks, dtype=jnp.int32)
    local = block_slot < row_blocks
    peer = (block_slot - row_blocks) // CAP
    place = (block_slot - row_blocks) % CAP
    came = jnp.where(local, block_slot, row_blocks + ((me - peer - 1) % doms) * CAP + place)
    goes = jnp.where(local, -1, ((peer - me - 1) % doms) * CAP + place)
    slots = jnp.arange(doms * CAP, dtype=jnp.int32)
    entry_of = jnp.sum(jnp.where(goes[None, :] == slots[:, None], entry[None, :], 0), axis=1)
    count = jnp.sum((block_slot[None, :] == blocks[:, None]).astype(jnp.int32), axis=1)
    pairs = (count + 1) // 2
    first = jnp.sum(jnp.where(blocks[None, :] < blocks[:, None], pairs[None, :], 0), axis=1)
    before = jnp.sum(jnp.where(blocks[None, :] < block_slot[:, None], pairs[None, :], 0), axis=1)
    same = (block_slot[None, :] == block_slot[:, None]) & (entry[None, :] < entry[:, None])
    rank = jnp.sum(same.astype(jnp.int32), axis=1)
    at = jnp.where(local, 2 * before + rank, -1)
    spots = jnp.arange(2 * chunks, dtype=jnp.int32)
    order = jnp.sum(jnp.where(at[None, :] == spots[:, None], entry[None, :] + 1, 0), axis=1) - 1
    chunk = jnp.arange(chunks, dtype=jnp.int32)
    starts = (first[None, :] == chunk[:, None]) & (count[None, :] > 0)
    keep = 1 - jnp.max(starts.astype(jnp.int32), axis=1)
    last = jnp.where(count > 0, first + pairs - 1, chunks)
    used = jnp.maximum(order, 0)
    lists = (
        came,
        entry_of // 2,
        entry_of % 2,
        entry_of // 8,
        used // 2,
        jnp.where(order < 0, 2, order % 2),
        used // 8,
        keep,
        last,
    )
    return jnp.concatenate([x.astype(jnp.int32) for x in lists]), chunks


def kernel(
    doms,
    cols,
    classes,
    chunks,
    index,
    features,
    w_hidden,
    w_out,
    tiles,
    request,
    code,
    prop_out,
    grad_out,
    head_send,
    stat_send,
    stat_recv,
    want,
    want_s,
    teleports,
    table0,
    table1,
    table2,
    swapped,
    inverse,
    final,
    grad,
    w_plain,
    w_swapped,
    acc,
    come_in,
    remote_tiles,
    local_tiles,
    route,
    out_buf,
    back_buf,
    head_sems,
    stat_sems,
    request_sems,
    local_sem,
    send_sems,
    recv_sems,
):
    me = lax.axis_index("dom")
    my_col = lax.axis_index("col")
    row_blocks = code.shape[0]
    entries = row_blocks * 8
    share = w_out.shape[1] // cols
    mine = features.shape[0] // BLOCK
    slots, spots = doms * CAP, 2 * chunks
    at_slot_tile = entries
    at_slot_half = at_slot_tile + slots
    at_slot_row = at_slot_half + slots
    at_tile = at_slot_row + slots
    at_half = at_tile + spots
    at_row = at_half + spots
    at_keep = at_row + spots
    at_last = at_keep + chunks
    peers = doms - 1
    local_rows = row_blocks * HALF
    table = (table0, table1, table2)

    lane = lax.broadcasted_iota(jnp.int32, (HALF, LANES), 1)
    low = lane < BLOCK

    def swap(x):
        return pltpu.roll(x, BLOCK, 1)

    def dom_at(shift):
        return lax.rem(me + shift, doms)

    def col_at(shift):
        return lax.rem(my_col + shift, cols)

    barrier = pltpu.get_barrier_semaphore()

    def greet_dom(k, carry):
        pl.semaphore_signal(barrier, inc=1, device_id={"dom": dom_at(k + 1)}, device_id_type=pl.DeviceIdType.MESH)
        return carry

    def greet_col(k, carry):
        pl.semaphore_signal(barrier, inc=1, device_id={"col": col_at(k + 1)}, device_id_type=pl.DeviceIdType.MESH)
        return carry

    lax.fori_loop(0, peers, greet_dom, 0)
    lax.fori_loop(0, cols - 1, greet_col, 0)

    hidden = jax.nn.relu(jnp.dot(features[...], w_hidden[...], preferred_element_type=F32)).astype(BF16)
    heads = jnp.dot(hidden, w_out[...], preferred_element_type=F32).T
    for c in range(cols):
        for pair in range(mine // 2):
            part = heads[c * share : (c + 1) * share, pair * LANES : (pair + 1) * LANES]
            top, bottom = part[:HALF], part[HALF:]
            at = c * mine + pair * 2
            head_send[at] = jnp.where(low, top, swap(bottom)).astype(BF16)
            head_send[at + 1] = jnp.where(low, swap(top), bottom).astype(BF16)

    pl.semaphore_wait(barrier, peers + cols - 1)

    def request_copy(k):
        return pltpu.make_async_remote_copy(
            src_ref=request.at[dom_at(k + 1)],
            dst_ref=want.at[k],
            send_sem=request_sems.at[0],
            recv_sem=request_sems.at[1],
            device_id={"dom": dom_at(k + 1)},
            device_id_type=pl.DeviceIdType.MESH,
        )

    def start_request(k, carry):
        request_copy(k).start()
        return carry

    lax.fori_loop(0, peers, start_request, 0)

    def own(col):
        return pl.ds(col * mine, mine)

    def head_copy(j):
        return pltpu.make_async_remote_copy(
            src_ref=head_send.at[own(col_at(j + 1))],
            dst_ref=teleports.at[own(my_col)],
            send_sem=head_sems.at[0, j],
            recv_sem=head_sems.at[1, j],
            device_id={"col": col_at(j + 1)},
            device_id_type=pl.DeviceIdType.MESH,
        )

    for j in range(cols - 1):
        head_copy(j).start()
    teleports[own(my_col)] = head_send[own(my_col)]

    def row_tiles(r):
        parts = [tiles[4 * r + q] for q in range(4)]
        return jnp.concatenate(parts, axis=1)

    ones = jnp.ones((HALF, 4 * LANES), BF16)
    contract_lanes = (((1,), (1,)), ((), ()))

    def degree(r, carry):
        sums = lax.dot_general(ones, row_tiles(r), contract_lanes, preferred_element_type=F32)
        inverse[r] = 1.0 / (1.0 + jnp.concatenate([sums, sums], axis=1))
        return carry

    lax.fori_loop(0, row_blocks, degree, 0, unroll=4)

    def all_requests(wait):
        whole = pltpu.make_async_remote_copy(
            src_ref=want.at[pl.ds(0, peers)],
            dst_ref=want.at[pl.ds(0, peers)],
            send_sem=request_sems.at[0],
            recv_sem=request_sems.at[1],
            device_id={"dom": dom_at(1)},
            device_id_type=pl.DeviceIdType.MESH,
        )
        whole.wait_recv() if wait == "recv" else whole.wait_send()

    all_requests("recv")
    want[peers] = jnp.full((1, LANES), row_blocks, jnp.int32)
    teleports[row_blocks] = jnp.zeros((HALF, LANES), BF16)
    w_plain[row_blocks] = jnp.zeros((HALF, LANES), BF16)
    to_scalars = pltpu.make_async_copy(want, want_s, local_sem.at[0])
    to_scalars.start()
    to_scalars.wait()

    for j in range(cols - 1):
        head_copy(j).wait_recv()

    def swap_first(r, carry):
        block = teleports[r]
        table0[r] = block
        swapped[0, r] = swap(block.astype(F32)).astype(BF16)
        return carry

    lax.fori_loop(0, row_blocks, swap_first, 0, unroll=4)

    def peer_copy(step, k):
        at = pl.ds(k * CAP, CAP)
        if step < STEPS:
            dst = table[step].at[pl.ds(row_blocks + k * CAP, CAP)]
        else:
            dst = back_buf.at[step - STEPS, at]
        return pltpu.make_async_remote_copy(
            src_ref=out_buf.at[step, at],
            dst_ref=dst,
            send_sem=send_sems.at[step],
            recv_sem=recv_sems.at[step],
            device_id={"dom": dom_at(k + 1)},
            device_id_type=pl.DeviceIdType.MESH,
        )

    def whole_copy(step):
        at = pl.ds(0, peers * CAP)
        dst = table[step].at[pl.ds(row_blocks, peers * CAP)] if step < STEPS else back_buf.at[step - STEPS, at]
        return pltpu.make_async_remote_copy(
            src_ref=out_buf.at[step, at],
            dst_ref=dst,
            send_sem=send_sems.at[step],
            recv_sem=recv_sems.at[step],
            device_id={"dom": dom_at(1)},
            device_id_type=pl.DeviceIdType.MESH,
        )

    def two_blocks(plain, turned, a, b):
        top = jnp.where(low, plain(a), turned(b))
        bottom = jnp.where(low, turned(a), plain(b))
        return jnp.concatenate([top, bottom], axis=0)

    side = jnp.where(lax.broadcasted_iota(jnp.int32, (BLOCK, LANES), 1) < BLOCK, 0, 1)

    def build_tiles(dst, n, start, half):
        pair = tiles[start].astype(F32)
        tile = jnp.where(side == half, pair, jnp.where(side == 1 - half, swap(pair), 0.0))
        dst[pl.ds(pl.multiple_of(n * BLOCK, BLOCK), BLOCK), :] = tile.astype(BF16)

    def build_remote(n, carry):
        build_tiles(remote_tiles, n, index[at_slot_tile + n], index[at_slot_half + n])
        return carry

    def build_local(n, carry):
        build_tiles(local_tiles, n, index[at_tile + n], index[at_half + n])
        return carry

    def build_route(m, carry):
        row = lax.broadcasted_iota(jnp.int32, (local_rows, LANES), 0)
        col = lax.broadcasted_iota(jnp.int32, (local_rows, LANES), 1)
        wide = lax.broadcasted_iota(jnp.int32, (1, LANES), 1) < BLOCK
        target = jnp.where(wide, want[2 * m], want[2 * m + 1])
        hit = row - col % HALF == target * HALF
        at = pl.ds(pl.multiple_of(m * local_rows, local_rows), local_rows)
        route[at, :] = jnp.where(hit, 1.0, 0.0).astype(BF16)
        return carry

    for step in range(STEPS):
        state_at = teleports if step == 0 else w_plain

        def send(k, carry):
            for c in range(CAP):
                block = want_s[peers - 1 - k, 0, HALF * c]
                out_buf[step, k * CAP + c] = state_at[block]
            peer_copy(step, k).start()
            return carry

        lax.fori_loop(0, peers, send, 0)
        if step == 0:
            lax.fori_loop(0, 2 * chunks, build_local, 0, unroll=2)
        elif step == 1:
            lax.fori_loop(0, peers * CAP, build_remote, 0, unroll=2)
        else:
            lax.fori_loop(0, doms // 2, build_route, 0)
            acc[chunks] = jnp.zeros((HALF, LANES), F32)
            for late in range(STEPS):
                back_buf[late, pl.ds(peers * CAP, CAP)] = jnp.zeros((CAP, HALF, LANES), BF16)
        whole_copy(step).wait_recv()

        def swap_remote(k, carry):
            at = row_blocks + k
            swapped[step, at] = swap(table[step][at].astype(F32)).astype(BF16)
            return carry

        lax.fori_loop(0, peers * CAP, swap_remote, 0, unroll=4)

        def plain(i):
            return table[step][i]

        def turned(i):
            return swapped[step, i]

        def propagate(r, carry):
            picked = [two_blocks(plain, turned, index[8 * r + 2 * q], index[8 * r + 2 * q + 1]) for q in range(4)]
            sums = lax.dot_general(
                jnp.concatenate(picked, axis=1), row_tiles(r), contract_lanes, preferred_element_type=F32
            )
            sums = jnp.concatenate([sums[:HALF], sums[HALF:]], axis=1)
            rounded = state_at[r].astype(F32)
            teleport = teleports[r].astype(F32)
            state = (1.0 - TELEPORT) * ((sums + rounded) * inverse[r]) + TELEPORT * teleport
            if step + 1 < STEPS:
                table[step + 1][r] = state.astype(BF16)
                w_plain[r] = state.astype(BF16)
                swapped[step + 1, r] = swap(state).astype(BF16)
            else:
                final[r] = state
            return carry

        lax.fori_loop(0, row_blocks, propagate, 0, unroll=4)

    low_row = lax.broadcasted_iota(jnp.int32, (1, LANES), 1) < BLOCK
    class_id = (
        my_col * share
        + lax.broadcasted_iota(jnp.int32, (HALF, LANES), 0)
        + jnp.where(low, 0, HALF)
    )
    usable = class_id < classes

    def statistics(r, carry):
        state = final[r]
        top = jnp.max(jnp.where(usable, state, FILL), axis=0, keepdims=True)
        top = jnp.maximum(top, swap(top))
        expo = jnp.where(usable, jnp.exp(state - top), 0.0)
        sums = jnp.sum(expo, axis=0, keepdims=True)
        sums = sums + swap(sums)
        stat_send[pl.ds(r, 1), :] = jnp.where(low_row, top, sums)
        return carry

    lax.fori_loop(0, row_blocks, statistics, 0, unroll=4)

    def stat_copy(j):
        return pltpu.make_async_remote_copy(
            src_ref=stat_send,
            dst_ref=stat_recv.at[j],
            send_sem=stat_sems.at[0, j],
            recv_sem=stat_sems.at[1, j],
            device_id={"col": col_at(j + 1)},
            device_id_type=pl.DeviceIdType.MESH,
        )

    for j in range(cols - 1):
        stat_copy(j).start()

    def unpack(source, dest):
        def pair(m, carry):
            first, second = source[2 * m], source[2 * m + 1]
            at = pl.ds(pl.multiple_of(m * LANES, LANES), LANES)
            dest[pl.ds(0, HALF), at] = jnp.where(low, first, swap(second))
            dest[pl.ds(HALF, HALF), at] = jnp.where(low, swap(first), second)
            return carry

        lax.fori_loop(0, row_blocks // 2, pair, 0, unroll=2)

    unpack(final, prop_out)
    for j in range(cols - 1):
        stat_copy(j).wait_recv()

    wide_low = lax.broadcasted_iota(jnp.int32, (row_blocks, LANES), 1) < BLOCK
    stats = [stat_send[...]] + [stat_recv[j] for j in range(cols - 1)]
    tops = [jnp.where(wide_low, s, swap(s)) for s in stats]
    sums = [jnp.where(wide_low, swap(s), s) for s in stats]
    top = functools.reduce(jnp.maximum, tops)
    whole = functools.reduce(jnp.add, [s * jnp.exp(t - top) for s, t in zip(sums, tops)])
    stat_send_free = [stat_copy(j) for j in range(cols - 1)]
    for copy in stat_send_free:
        copy.wait_send()
    stat_send[...] = top
    stat_recv[0] = 1.0 / whole

    def store_scaled(r, gradient):
        scaled = inverse[r] * gradient
        w_plain[r] = scaled.astype(BF16)
        w_swapped[r] = swap(scaled).astype(BF16)

    def cotangent(r, carry):
        state = final[r]
        expo = jnp.exp(state - stat_send[pl.ds(r, 1), :])
        probs = expo * stat_recv[0, pl.ds(r, 1), :]
        coded = code[r]
        onehot = jnp.where(class_id == coded % 256, 1.0, 0.0)
        weight = (coded // 256).astype(F32)
        gradient = jnp.where(usable, weight * (probs - onehot), 0.0)
        grad[r] = TELEPORT * gradient
        store_scaled(r, gradient)
        return carry

    lax.fori_loop(0, row_blocks, cotangent, 0, unroll=2)

    nothing = jnp.zeros((HALF, LANES), BF16)

    def w_at(i):
        return w_plain[i]

    def w_turned(i):
        return w_swapped[i]

    for late in range(STEPS):

        def send_back(k, carry):
            lines = []
            for c in range(CAP):
                r = index[at_slot_row + CAP * k + c]
                if c % 2 == 0:
                    top, bottom = jnp.where(low, w_at(r), nothing), jnp.where(low, w_turned(r), nothing)
                else:
                    top, bottom = jnp.where(low, nothing, w_turned(r)), jnp.where(low, nothing, w_at(r))
                here = jnp.concatenate([top, bottom], axis=0)
                blank = jnp.zeros_like(here)
                lines.append(jnp.concatenate([here, blank] if c < 2 else [blank, here], axis=1))
            weights = remote_tiles[pl.ds(pl.multiple_of(k * CAP * BLOCK, CAP * BLOCK), CAP * BLOCK), :]
            products = jnp.dot(jnp.concatenate(lines, axis=0), weights, preferred_element_type=F32)
            for c in range(CAP):
                top = products[2 * c * HALF : (2 * c + 1) * HALF]
                bottom = products[(2 * c + 1) * HALF : (2 * c + 2) * HALF]
                out_buf[STEPS + late, k * CAP + c] = jnp.where(low, top, bottom).astype(BF16)
            peer_copy(STEPS + late, k).start()
            return carry

        lax.fori_loop(0, peers, send_back, 0)

        def local_chunk(m, running):
            a, b = index[at_row + 2 * m], index[at_row + 2 * m + 1]
            weights = local_tiles[pl.ds(pl.multiple_of(m * 2 * BLOCK, 2 * BLOCK), 2 * BLOCK), :]
            products = jnp.dot(two_blocks(w_at, w_turned, a, b), weights, preferred_element_type=F32)
            term = jnp.where(low, products[:HALF], products[HALF:])
            running = running * index[at_keep + m].astype(F32) + term
            acc[m] = running
            return running

        lax.fori_loop(0, chunks, local_chunk, jnp.zeros((HALF, LANES), F32), unroll=4)

        def local_sum(r, carry):
            come_in[r] = acc[index[at_last + r]]
            return carry

        lax.fori_loop(0, row_blocks, local_sum, 0, unroll=4)
        whole_copy(STEPS + late).wait_recv()

        def arrive(m, carry):
            left = route[pl.ds(pl.multiple_of(2 * m * local_rows, local_rows), local_rows), :]
            right = route[pl.ds(pl.multiple_of((2 * m + 1) * local_rows, local_rows), local_rows), :]
            part = back_buf[late, pl.ds(m * 4 * CAP, 4 * CAP)].reshape(4 * PEER, LANES)
            sums = jnp.dot(jnp.concatenate([left, right], axis=1), part, preferred_element_type=F32)
            come_in[...] += sums.reshape(row_blocks, HALF, LANES)
            return carry

        lax.fori_loop(0, doms // 4, arrive, 0)

        def finish(r, carry):
            gradient = (1.0 - TELEPORT) * (come_in[r] + w_plain[r].astype(F32))
            if late < STEPS - 1:
                grad[r] += TELEPORT * gradient
                store_scaled(r, gradient)
            else:
                grad[r] += gradient
            return carry

        lax.fori_loop(0, row_blocks, finish, 0, unroll=4)

    unpack(grad, grad_out)

    all_requests("send")
    for j in range(cols - 1):
        head_copy(j).wait_send()
    for step in range(2 * STEPS):
        whole_copy(step).wait_send()


def body(features, w_hidden, w_out, block_values, block_slot, requested, labels, train_mask):
    doms, cols = lax.axis_size("dom"), lax.axis_size("col")
    nodes = labels.shape[0]
    row_blocks = nodes // BLOCK
    share = w_out.shape[1] // cols
    entries = block_slot.shape[0]
    index, chunks = index_tables(block_slot, doms, row_blocks)
    tiles = (
        block_values.reshape(entries // 2, 2, BLOCK, BLOCK).transpose(0, 2, 1, 3).reshape(entries // 2, BLOCK, LANES)
    )
    asked = jnp.where(requested < 0, row_blocks, requested)
    request = jnp.broadcast_to(asked.reshape(doms, 1, 1, CAP, 1), (doms, 1, 2, CAP, HALF)).reshape(doms, 1, LANES)
    code = (labels + 256 * train_mask).reshape(row_blocks, 1, 1, BLOCK)
    code = jnp.broadcast_to(code, (row_blocks, 1, 2, BLOCK)).reshape(row_blocks, 1, LANES)
    peers = doms - 1
    local_rows = row_blocks * HALF
    all_blocks = row_blocks + doms * CAP
    vmem, dma = pltpu.VMEM, pltpu.SemaphoreType.DMA
    mine = features.shape[0] // BLOCK
    in_vmem = pl.BlockSpec(memory_space=pltpu.VMEM)
    return pl.pallas_call(
        functools.partial(kernel, doms, cols, NCLASS, chunks),
        out_shape=[jax.ShapeDtypeStruct((share, nodes), F32)] * 2,
        in_specs=[pl.BlockSpec(memory_space=pltpu.SMEM)] + [in_vmem] * 6,
        out_specs=[in_vmem] * 2,
        scratch_shapes=[
            vmem((cols * mine, HALF, LANES), BF16),
            vmem((row_blocks, LANES), F32),
            vmem((cols - 1, row_blocks, LANES), F32),
            vmem((doms, 1, LANES), jnp.int32),
            pltpu.SMEM((doms, 1, LANES), jnp.int32),
            vmem((row_blocks + 1, HALF, LANES), BF16),
            vmem((all_blocks, HALF, LANES), BF16),
            vmem((all_blocks, HALF, LANES), BF16),
            vmem((all_blocks, HALF, LANES), BF16),
            vmem((STEPS, all_blocks, HALF, LANES), BF16),
            vmem((row_blocks, HALF, LANES), F32),
            vmem((row_blocks, HALF, LANES), F32),
            vmem((row_blocks, HALF, LANES), F32),
            vmem((row_blocks + 1, HALF, LANES), BF16),
            vmem((row_blocks, HALF, LANES), BF16),
            vmem((chunks + 1, HALF, LANES), F32),
            vmem((row_blocks, HALF, LANES), F32),
            vmem((peers * CAP * BLOCK, LANES), BF16),
            vmem((2 * chunks * BLOCK, LANES), BF16),
            vmem((doms // 2 * local_rows, LANES), BF16),
            vmem((2 * STEPS, peers * CAP, HALF, LANES), BF16),
            vmem((STEPS, doms * CAP, HALF, LANES), BF16),
            dma((2, cols - 1)),
            dma((2, cols - 1)),
            dma((2,)),
            dma((1,)),
            dma((2 * STEPS,)),
            dma((2 * STEPS,)),
        ],
        compiler_params=pltpu.CompilerParams(
            collective_id=0, has_side_effects=True, vmem_limit_bytes=48 * 2**20
        ),
    )(index, features, w_hidden, w_out, tiles, request, code)


def solution(mesh):
    return jax.shard_map(
        body,
        mesh=mesh,
        in_specs=(
            P(("dom", "col"), None),
            P(),
            P(),
            P("dom", None),
            P("dom"),
            P("dom", None, None),
            P("dom"),
            P("dom"),
        ),
        out_specs=(P("col", "dom"), P("col", "dom")),
        check_vma=False,
    )
```

```python
import functools

import jax
import jax.numpy as jnp
from jax import lax
from jax.experimental import pallas as pl
from jax.experimental.pallas import tpu as pltpu
from jax.sharding import PartitionSpec as P

NCLASS = 172
BLOCK = 64
STEPS = 3
CAP = 4
TELEPORT = 0.1
FILL = -1e30

HALF = 16
LANES = 128
PEER = CAP * HALF
GROUP = 8

F32 = jnp.float32
BF16 = jnp.bfloat16


def index_tables(block_slot, doms, row_blocks):
    entries = block_slot.shape[0]
    me = lax.axis_index("dom")
    chunks = -(-((entries - (doms - 1) + row_blocks) // 2) // GROUP) * GROUP
    entry = jnp.arange(entries, dtype=jnp.int32)
    blocks = jnp.arange(row_blocks, dtype=jnp.int32)
    local = block_slot < row_blocks
    peer = (block_slot - row_blocks) // CAP
    place = (block_slot - row_blocks) % CAP
    came = jnp.where(local, block_slot, row_blocks + ((me - peer - 1) % doms) * CAP + place)
    goes = jnp.where(local, -1, ((peer - me - 1) % doms) * CAP + place)
    slots = jnp.arange(doms * CAP, dtype=jnp.int32)
    entry_of = jnp.sum(jnp.where(goes[None, :] == slots[:, None], entry[None, :], 0), axis=1)
    count = jnp.sum((block_slot[None, :] == blocks[:, None]).astype(jnp.int32), axis=1)
    pairs = (count + 1) // 2
    first = jnp.sum(jnp.where(blocks[None, :] < blocks[:, None], pairs[None, :], 0), axis=1)
    before = jnp.sum(jnp.where(blocks[None, :] < block_slot[:, None], pairs[None, :], 0), axis=1)
    same = (block_slot[None, :] == block_slot[:, None]) & (entry[None, :] < entry[:, None])
    rank = jnp.sum(same.astype(jnp.int32), axis=1)
    at = jnp.where(local, 2 * before + rank, -1)
    spots = jnp.arange(2 * chunks, dtype=jnp.int32)
    order = jnp.sum(jnp.where(at[None, :] == spots[:, None], entry[None, :] + 1, 0), axis=1) - 1
    chunk = jnp.arange(chunks, dtype=jnp.int32)
    starts = (first[None, :] == chunk[:, None]) & (count[None, :] > 0)
    keep = 1 - jnp.max(starts.astype(jnp.int32), axis=1)
    last = jnp.where(count > 0, first + pairs - 1, chunks)
    used = jnp.maximum(order, 0)
    lists = (
        came,
        entry_of // 2,
        entry_of % 2,
        entry_of // 8,
        used // 2,
        jnp.where(order < 0, 2, order % 2),
        used // 8,
        keep,
        last,
    )
    return jnp.concatenate([x.astype(jnp.int32) for x in lists]), chunks


def kernel(
    doms,
    cols,
    classes,
    chunks,
    index,
    features,
    w_hidden,
    w_out,
    tiles,
    request,
    code,
    prop_out,
    grad_out,
    head_send,
    stat_send,
    stat_recv,
    want,
    want_s,
    teleports,
    table0,
    table1,
    table2,
    swapped0,
    swapped1,
    swapped2,
    inverse,
    final,
    grad,
    w_plain,
    w_swapped,
    acc,
    come_in,
    remote_tiles,
    local_tiles,
    route,
    out_buf,
    back_buf,
    head_sems,
    stat_sems,
    request_sems,
    local_sem,
    send_sems,
    recv_sems,
):
    me = lax.axis_index("dom")
    my_col = lax.axis_index("col")
    row_blocks = code.shape[0]
    entries = row_blocks * 8
    share = w_out.shape[1] // cols
    mine = features.shape[0] // BLOCK
    slots, spots = doms * CAP, 2 * chunks
    at_slot_tile = entries
    at_slot_half = at_slot_tile + slots
    at_slot_row = at_slot_half + slots
    at_tile = at_slot_row + slots
    at_half = at_tile + spots
    at_row = at_half + spots
    at_keep = at_row + spots
    at_last = at_keep + chunks
    peers = doms - 1
    local_rows = row_blocks * HALF
    table = (table0, table1, table2)
    swapped = (swapped0, swapped1, swapped2)

    lane = lax.broadcasted_iota(jnp.int32, (HALF, LANES), 1)
    low = lane < BLOCK

    def swap(x):
        return pltpu.roll(x, BLOCK, 1)

    def dom_at(shift):
        return lax.rem(me + shift, doms)

    def col_at(shift):
        return lax.rem(my_col + shift, cols)

    barrier = pltpu.get_barrier_semaphore()

    def greet_dom(k, carry):
        pl.semaphore_signal(barrier, inc=1, device_id={"dom": dom_at(k + 1)}, device_id_type=pl.DeviceIdType.MESH)
        return carry

    def greet_col(k, carry):
        pl.semaphore_signal(barrier, inc=1, device_id={"col": col_at(k + 1)}, device_id_type=pl.DeviceIdType.MESH)
        return carry

    lax.fori_loop(0, peers, greet_dom, 0)
    lax.fori_loop(0, cols - 1, greet_col, 0)

    hidden = jax.nn.relu(jnp.dot(features[...], w_hidden[...], preferred_element_type=F32)).astype(BF16)
    heads = jnp.dot(hidden, w_out[...], preferred_element_type=F32).T
    for c in range(cols):
        for pair in range(mine // 2):
            part = heads[c * share : (c + 1) * share, pair * LANES : (pair + 1) * LANES]
            top, bottom = part[:HALF], part[HALF:]
            at = c * mine + pair * 2
            head_send[at] = jnp.where(low, top, swap(bottom)).astype(BF16)
            head_send[at + 1] = jnp.where(low, swap(top), bottom).astype(BF16)

    pl.semaphore_wait(barrier, peers + cols - 1)

    def request_copy(k):
        return pltpu.make_async_remote_copy(
            src_ref=request.at[dom_at(k + 1)],
            dst_ref=want.at[k],
            send_sem=request_sems.at[0],
            recv_sem=request_sems.at[1],
            device_id={"dom": dom_at(k + 1)},
            device_id_type=pl.DeviceIdType.MESH,
        )

    def start_request(k, carry):
        request_copy(k).start()
        return carry

    lax.fori_loop(0, peers, start_request, 0)

    def own(col):
        return pl.ds(col * mine, mine)

    def head_copy(j):
        return pltpu.make_async_remote_copy(
            src_ref=head_send.at[own(col_at(j + 1))],
            dst_ref=teleports.at[own(my_col)],
            send_sem=head_sems.at[0, j],
            recv_sem=head_sems.at[1, j],
            device_id={"col": col_at(j + 1)},
            device_id_type=pl.DeviceIdType.MESH,
        )

    for j in range(cols - 1):
        head_copy(j).start()
    teleports[own(my_col)] = head_send[own(my_col)]

    def row_tiles(r):
        parts = [tiles[4 * r + q] for q in range(4)]
        return jnp.concatenate(parts, axis=1)

    ones = jnp.ones((HALF, 4 * LANES), BF16)
    contract_lanes = (((1,), (1,)), ((), ()))

    def degree(r, carry):
        sums = lax.dot_general(ones, row_tiles(r), contract_lanes, preferred_element_type=F32)
        inverse[r] = 1.0 / (1.0 + jnp.concatenate([sums, sums], axis=1))
        return carry

    lax.fori_loop(0, row_blocks, degree, 0, unroll=4)

    def all_requests(wait):
        whole = pltpu.make_async_remote_copy(
            src_ref=want.at[pl.ds(0, peers)],
            dst_ref=want.at[pl.ds(0, peers)],
            send_sem=request_sems.at[0],
            recv_sem=request_sems.at[1],
            device_id={"dom": dom_at(1)},
            device_id_type=pl.DeviceIdType.MESH,
        )
        whole.wait_recv() if wait == "recv" else whole.wait_send()

    all_requests("recv")
    want[peers] = jnp.full((1, LANES), row_blocks, jnp.int32)
    teleports[row_blocks] = jnp.zeros((HALF, LANES), BF16)
    w_plain[row_blocks] = jnp.zeros((HALF, LANES), BF16)
    to_scalars = pltpu.make_async_copy(want, want_s, local_sem.at[0])
    to_scalars.start()
    to_scalars.wait()

    for j in range(cols - 1):
        head_copy(j).wait_recv()

    def turn(blocks):
        count = blocks.shape[0]
        flat = swap(blocks.astype(F32).reshape(count * HALF, LANES))
        return flat.astype(BF16).reshape(count, HALF, LANES)

    def swap_first(group, carry):
        at = pl.ds(group * GROUP, GROUP)
        blocks = teleports[at]
        table0[at] = blocks
        swapped[0][at] = turn(blocks)
        return carry

    lax.fori_loop(0, row_blocks // GROUP, swap_first, 0)

    def peer_copy(step, k):
        at = pl.ds(k * CAP, CAP)
        if step < STEPS:
            dst = table[step].at[pl.ds(row_blocks + k * CAP, CAP)]
        else:
            dst = back_buf.at[step - STEPS, at]
        return pltpu.make_async_remote_copy(
            src_ref=out_buf.at[step, at],
            dst_ref=dst,
            send_sem=send_sems.at[step],
            recv_sem=recv_sems.at[step],
            device_id={"dom": dom_at(k + 1)},
            device_id_type=pl.DeviceIdType.MESH,
        )

    def whole_copy(step):
        at = pl.ds(0, peers * CAP)
        dst = table[step].at[pl.ds(row_blocks, peers * CAP)] if step < STEPS else back_buf.at[step - STEPS, at]
        return pltpu.make_async_remote_copy(
            src_ref=out_buf.at[step, at],
            dst_ref=dst,
            send_sem=send_sems.at[step],
            recv_sem=recv_sems.at[step],
            device_id={"dom": dom_at(1)},
            device_id_type=pl.DeviceIdType.MESH,
        )

    def two_blocks(plain, turned, a, b):
        top = jnp.where(low, plain(a), turned(b))
        bottom = jnp.where(low, turned(a), plain(b))
        return jnp.concatenate([top, bottom], axis=0)

    side = jnp.where(lax.broadcasted_iota(jnp.int32, (BLOCK, LANES), 1) < BLOCK, 0, 1)

    def built(start, half):
        pair = tiles[start].astype(F32)
        return jnp.where(side == half, pair, jnp.where(side == 1 - half, swap(pair), 0.0)).astype(BF16)

    def build_tiles(dst, group, at_start, at_side):
        first = group * 4
        made = [built(index[at_start + first + i], index[at_side + first + i]) for i in range(4)]
        at = pl.ds(pl.multiple_of(first * BLOCK, 4 * BLOCK), 4 * BLOCK)
        dst[at, :] = jnp.concatenate(made, axis=0)

    def build_remote(group, carry):
        build_tiles(remote_tiles, group, at_slot_tile, at_slot_half)
        return carry

    def build_local(group, carry):
        build_tiles(local_tiles, group, at_tile, at_half)
        return carry

    def build_route(m, carry):
        row = lax.broadcasted_iota(jnp.int32, (local_rows, LANES), 0)
        col = lax.broadcasted_iota(jnp.int32, (local_rows, LANES), 1)
        wide = lax.broadcasted_iota(jnp.int32, (1, LANES), 1) < BLOCK
        target = jnp.where(wide, want[2 * m], want[2 * m + 1])
        hit = row - col % HALF == target * HALF
        at = pl.ds(pl.multiple_of(m * local_rows, local_rows), local_rows)
        route[at, :] = jnp.where(hit, 1.0, 0.0).astype(BF16)
        return carry

    for step in range(STEPS):
        state_at = teleports if step == 0 else w_plain

        def send(k, carry):
            for c in range(CAP):
                block = want_s[peers - 1 - k, 0, HALF * c]
                out_buf[step, k * CAP + c] = state_at[block]
            peer_copy(step, k).start()
            return carry

        lax.fori_loop(0, peers, send, 0)
        if step == 0:
            lax.fori_loop(0, chunks // 2, build_local, 0)
        elif step == 1:
            lax.fori_loop(0, peers, build_remote, 0)
        else:
            lax.fori_loop(0, doms // 2, build_route, 0)
            acc[chunks] = jnp.zeros((HALF, LANES), F32)
            for late in range(STEPS):
                back_buf[late, pl.ds(peers * CAP, CAP)] = jnp.zeros((CAP, HALF, LANES), BF16)
        whole_copy(step).wait_recv()

        def swap_remote(at):
            swapped[step][at] = turn(table[step][at])

        def swap_group(group, carry):
            swap_remote(pl.ds(row_blocks + group * 2 * GROUP, 2 * GROUP))
            return carry

        whole_groups = peers * CAP // (2 * GROUP)
        lax.fori_loop(0, whole_groups, swap_group, 0)
        swap_remote(pl.ds(row_blocks + whole_groups * 2 * GROUP, peers * CAP - whole_groups * 2 * GROUP))

        def plain(i):
            return table[step][i]

        def turned(i):
            return swapped[step][i]

        def propagate(group, carry):
            rows = [group * GROUP + i for i in range(GROUP)]
            sums = []
            for r in rows:
                picked = [two_blocks(plain, turned, index[8 * r + 2 * q], index[8 * r + 2 * q + 1]) for q in range(4)]
                sums.append(
                    lax.dot_general(
                        jnp.concatenate(picked, axis=1), row_tiles(r), contract_lanes, preferred_element_type=F32
                    )
                )
            sums = jnp.stack([jnp.concatenate([x[:HALF], x[HALF:]], axis=1) for x in sums])
            at = pl.ds(group * GROUP, GROUP)
            rounded, teleport = state_at[at].astype(F32), teleports[at].astype(F32)
            state = (1.0 - TELEPORT) * ((sums + rounded) * inverse[at]) + TELEPORT * teleport
            if step + 1 < STEPS:
                blocks = state.astype(BF16)
                flipped = turn(blocks)
                table[step + 1][at] = blocks
                w_plain[at] = blocks
                swapped[step + 1][at] = flipped
            else:
                final[at] = state
            return carry

        lax.fori_loop(0, row_blocks // GROUP, propagate, 0)

    low_group = lax.broadcasted_iota(jnp.int32, (GROUP, LANES), 1) < BLOCK
    class_id = (
        my_col * share
        + lax.broadcasted_iota(jnp.int32, (HALF, LANES), 0)
        + jnp.where(low, 0, HALF)
    )
    usable = class_id < classes

    def statistics(group, carry):
        at = pl.ds(pl.multiple_of(group * GROUP, GROUP), GROUP)
        state = final[at]
        top = jnp.max(jnp.where(usable, state, FILL), axis=1)
        top = jnp.maximum(top, swap(top))
        expo = jnp.where(usable, jnp.exp(state - top[:, None, :]), 0.0)
        sums = jnp.sum(expo, axis=1)
        sums = sums + swap(sums)
        stat_send[at, :] = jnp.where(low_group, top, sums)
        return carry

    lax.fori_loop(0, row_blocks // GROUP, statistics, 0)

    def stat_copy(j):
        return pltpu.make_async_remote_copy(
            src_ref=stat_send,
            dst_ref=stat_recv.at[j],
            send_sem=stat_sems.at[0, j],
            recv_sem=stat_sems.at[1, j],
            device_id={"col": col_at(j + 1)},
            device_id_type=pl.DeviceIdType.MESH,
        )

    for j in range(cols - 1):
        stat_copy(j).start()

    def unpack(source, dest):
        def pair(m, carry):
            first, second = source[2 * m], source[2 * m + 1]
            at = pl.ds(pl.multiple_of(m * LANES, LANES), LANES)
            dest[pl.ds(0, HALF), at] = jnp.where(low, first, swap(second))
            dest[pl.ds(HALF, HALF), at] = jnp.where(low, swap(first), second)
            return carry

        lax.fori_loop(0, row_blocks // 2, pair, 0, unroll=2)

    unpack(final, prop_out)
    for j in range(cols - 1):
        stat_copy(j).wait_recv()

    wide_low = lax.broadcasted_iota(jnp.int32, (row_blocks, LANES), 1) < BLOCK
    stats = [stat_send[...]] + [stat_recv[j] for j in range(cols - 1)]
    tops = [jnp.where(wide_low, s, swap(s)) for s in stats]
    sums = [jnp.where(wide_low, swap(s), s) for s in stats]
    top = functools.reduce(jnp.maximum, tops)
    whole = functools.reduce(jnp.add, [s * jnp.exp(t - top) for s, t in zip(sums, tops)])
    stat_send_free = [stat_copy(j) for j in range(cols - 1)]
    for copy in stat_send_free:
        copy.wait_send()
    stat_send[...] = top
    stat_recv[0] = 1.0 / whole

    def store_scaled(at, gradient):
        scaled = (inverse[at] * gradient).astype(BF16)
        flipped = turn(scaled)
        w_plain[at] = scaled
        w_swapped[at] = flipped

    def cotangent(group, carry):
        at = pl.ds(pl.multiple_of(group * GROUP, GROUP), GROUP)
        expo = jnp.exp(final[at] - stat_send[at, :][:, None, :])
        probs = expo * stat_recv[0, at, :][:, None, :]
        coded = code[at]
        onehot = jnp.where(class_id == coded % 256, 1.0, 0.0)
        weight = (coded // 256).astype(F32)
        gradient = jnp.where(usable, weight * (probs - onehot), 0.0)
        grad[at] = TELEPORT * gradient
        store_scaled(at, gradient)
        return carry

    lax.fori_loop(0, row_blocks // GROUP, cotangent, 0)

    nothing = jnp.zeros((HALF, LANES), BF16)

    def w_at(i):
        return w_plain[i]

    def w_turned(i):
        return w_swapped[i]

    for late in range(STEPS):

        def products_for(k):
            lines = []
            for c in range(CAP):
                r = index[at_slot_row + CAP * k + c]
                if c % 2 == 0:
                    top, bottom = jnp.where(low, w_at(r), nothing), jnp.where(low, w_turned(r), nothing)
                else:
                    top, bottom = jnp.where(low, nothing, w_turned(r)), jnp.where(low, nothing, w_at(r))
                here = jnp.concatenate([top, bottom], axis=0)
                blank = jnp.zeros_like(here)
                lines.append(jnp.concatenate([here, blank] if c < 2 else [blank, here], axis=1))
            weights = remote_tiles[pl.ds(pl.multiple_of(k * CAP * BLOCK, CAP * BLOCK), CAP * BLOCK), :]
            products = jnp.dot(jnp.concatenate(lines, axis=0), weights, preferred_element_type=F32)
            products = products.reshape(CAP, 2, HALF, LANES)
            return jnp.where(low, products[:, 0], products[:, 1]).astype(BF16)

        def send_back(first, count):
            ready = [products_for(first + i) for i in range(count)]
            for i, blocks in enumerate(ready):
                out_buf[STEPS + late, pl.ds((first + i) * CAP, CAP)] = blocks
            for i in range(count):
                peer_copy(STEPS + late, first + i).start()

        def send_group(group, carry):
            send_back(group * 4, 4)
            return carry

        lax.fori_loop(0, peers // 4, send_group, 0)
        send_back(peers // 4 * 4, peers % 4)

        def local_chunks(group, running):
            terms = []
            for i in range(GROUP):
                m = group * GROUP + i
                a, b = index[at_row + 2 * m], index[at_row + 2 * m + 1]
                weights = local_tiles[pl.ds(pl.multiple_of(m * 2 * BLOCK, 2 * BLOCK), 2 * BLOCK), :]
                products = jnp.dot(two_blocks(w_at, w_turned, a, b), weights, preferred_element_type=F32)
                terms.append(jnp.where(low, products[:HALF], products[HALF:]))
            sums = []
            for i in range(GROUP):
                running = running * index[at_keep + group * GROUP + i].astype(F32) + terms[i]
                sums.append(running)
            acc[pl.ds(group * GROUP, GROUP)] = jnp.stack(sums)
            return running

        lax.fori_loop(0, chunks // GROUP, local_chunks, jnp.zeros((HALF, LANES), F32))

        def local_sum(group, carry):
            picked = [acc[index[at_last + group * GROUP + i]] for i in range(GROUP)]
            come_in[pl.ds(group * GROUP, GROUP)] = jnp.stack(picked)
            return carry

        lax.fori_loop(0, row_blocks // GROUP, local_sum, 0)
        whole_copy(STEPS + late).wait_recv()

        def arrive(m, carry):
            left = route[pl.ds(pl.multiple_of(2 * m * local_rows, local_rows), local_rows), :]
            right = route[pl.ds(pl.multiple_of((2 * m + 1) * local_rows, local_rows), local_rows), :]
            part = back_buf[late, pl.ds(m * 4 * CAP, 4 * CAP)].reshape(4 * PEER, LANES)
            sums = jnp.dot(jnp.concatenate([left, right], axis=1), part, preferred_element_type=F32)
            come_in[...] += sums.reshape(row_blocks, HALF, LANES)
            return carry

        lax.fori_loop(0, doms // 4, arrive, 0)

        def finish(group, carry):
            at = pl.ds(group * GROUP, GROUP)
            gradient = (1.0 - TELEPORT) * (come_in[at] + w_plain[at].astype(F32))
            if late < STEPS - 1:
                grad[at] += TELEPORT * gradient
                store_scaled(at, gradient)
            else:
                grad[at] += gradient
            return carry

        lax.fori_loop(0, row_blocks // GROUP, finish, 0)

    unpack(grad, grad_out)

    all_requests("send")
    for j in range(cols - 1):
        head_copy(j).wait_send()
    for step in range(2 * STEPS):
        whole_copy(step).wait_send()


def body(features, w_hidden, w_out, block_values, block_slot, requested, labels, train_mask):
    doms, cols = lax.axis_size("dom"), lax.axis_size("col")
    nodes = labels.shape[0]
    row_blocks = nodes // BLOCK
    share = w_out.shape[1] // cols
    entries = block_slot.shape[0]
    index, chunks = index_tables(block_slot, doms, row_blocks)
    tiles = (
        block_values.reshape(entries // 2, 2, BLOCK, BLOCK).transpose(0, 2, 1, 3).reshape(entries // 2, BLOCK, LANES)
    )
    asked = jnp.where(requested < 0, row_blocks, requested)
    request = jnp.broadcast_to(asked.reshape(doms, 1, 1, CAP, 1), (doms, 1, 2, CAP, HALF)).reshape(doms, 1, LANES)
    code = (labels + 256 * train_mask).reshape(row_blocks, 1, 1, BLOCK)
    code = jnp.broadcast_to(code, (row_blocks, 1, 2, BLOCK)).reshape(row_blocks, 1, LANES)
    peers = doms - 1
    local_rows = row_blocks * HALF
    all_blocks = row_blocks + doms * CAP
    vmem, dma = pltpu.VMEM, pltpu.SemaphoreType.DMA
    mine = features.shape[0] // BLOCK
    in_vmem = pl.BlockSpec(memory_space=pltpu.VMEM)
    return pl.pallas_call(
        functools.partial(kernel, doms, cols, NCLASS, chunks),
        out_shape=[jax.ShapeDtypeStruct((share, nodes), F32)] * 2,
        in_specs=[pl.BlockSpec(memory_space=pltpu.SMEM)] + [in_vmem] * 6,
        out_specs=[in_vmem] * 2,
        scratch_shapes=[
            vmem((cols * mine, HALF, LANES), BF16),
            vmem((row_blocks, LANES), F32),
            vmem((cols - 1, row_blocks, LANES), F32),
            vmem((doms, 1, LANES), jnp.int32),
            pltpu.SMEM((doms, 1, LANES), jnp.int32),
            vmem((row_blocks + 1, HALF, LANES), BF16),
            vmem((all_blocks, HALF, LANES), BF16),
            vmem((all_blocks, HALF, LANES), BF16),
            vmem((all_blocks, HALF, LANES), BF16),
            vmem((all_blocks, HALF, LANES), BF16),
            vmem((all_blocks, HALF, LANES), BF16),
            vmem((all_blocks, HALF, LANES), BF16),
            vmem((row_blocks, HALF, LANES), F32),
            vmem((row_blocks, HALF, LANES), F32),
            vmem((row_blocks, HALF, LANES), F32),
            vmem((row_blocks + 1, HALF, LANES), BF16),
            vmem((row_blocks, HALF, LANES), BF16),
            vmem((chunks + 1, HALF, LANES), F32),
            vmem((row_blocks, HALF, LANES), F32),
            vmem((peers * CAP * BLOCK, LANES), BF16),
            vmem((2 * chunks * BLOCK, LANES), BF16),
            vmem((doms // 2 * local_rows, LANES), BF16),
            vmem((2 * STEPS, peers * CAP, HALF, LANES), BF16),
            vmem((STEPS, doms * CAP, HALF, LANES), BF16),
            dma((2, cols - 1)),
            dma((2, cols - 1)),
            dma((2,)),
            dma((1,)),
            dma((2 * STEPS,)),
            dma((2 * STEPS,)),
        ],
        compiler_params=pltpu.CompilerParams(
            collective_id=0, has_side_effects=True, vmem_limit_bytes=48 * 2**20
        ),
    )(index, features, w_hidden, w_out, tiles, request, code)


def solution(mesh):
    return jax.shard_map(
        body,
        mesh=mesh,
        in_specs=(
            P(("dom", "col"), None),
            P(),
            P(),
            P("dom", None),
            P("dom"),
            P("dom", None, None),
            P("dom"),
            P("dom"),
        ),
        out_specs=(P("col", "dom"), P("col", "dom")),
        check_vma=False,
    )
```

```python
import functools

import jax
import jax.numpy as jnp
from jax import lax
from jax.experimental import pallas as pl
from jax.experimental.pallas import tpu as pltpu
from jax.sharding import PartitionSpec as P

NCLASS = 172
BLOCK = 64
STEPS = 3
CAP = 4
TELEPORT = 0.1
FILL = -1e30

HALF = 16
LANES = 128
PEER = CAP * HALF
SPREAD = 32
GROUP = 8

F32 = jnp.float32
BF16 = jnp.bfloat16


def index_tables(block_slot, doms, row_blocks):
    entries = block_slot.shape[0]
    me = lax.axis_index("dom")
    chunks = -(-((entries - (doms - 1) + row_blocks) // 2) // GROUP) * GROUP
    entry = jnp.arange(entries, dtype=jnp.int32)
    blocks = jnp.arange(row_blocks, dtype=jnp.int32)
    local = block_slot < row_blocks
    peer = (block_slot - row_blocks) // CAP
    place = (block_slot - row_blocks) % CAP
    came = jnp.where(local, block_slot, row_blocks + ((me - peer - 1) % doms) * CAP + place)
    goes = jnp.where(local, -1, ((peer - me - 1) % doms) * CAP + place)
    slots = jnp.arange(doms * CAP, dtype=jnp.int32)
    entry_of = jnp.sum(jnp.where(goes[None, :] == slots[:, None], entry[None, :], 0), axis=1)
    count = jnp.sum((block_slot[None, :] == blocks[:, None]).astype(jnp.int32), axis=1)
    pairs = (count + 1) // 2
    first = jnp.sum(jnp.where(blocks[None, :] < blocks[:, None], pairs[None, :], 0), axis=1)
    before = jnp.sum(jnp.where(blocks[None, :] < block_slot[:, None], pairs[None, :], 0), axis=1)
    same = (block_slot[None, :] == block_slot[:, None]) & (entry[None, :] < entry[:, None])
    rank = jnp.sum(same.astype(jnp.int32), axis=1)
    at = jnp.where(local, 2 * before + rank, -1)
    spots = jnp.arange(2 * chunks, dtype=jnp.int32)
    order = jnp.sum(jnp.where(at[None, :] == spots[:, None], entry[None, :] + 1, 0), axis=1) - 1
    chunk = jnp.arange(chunks, dtype=jnp.int32)
    starts = (first[None, :] == chunk[:, None]) & (count[None, :] > 0)
    keep = 1 - jnp.max(starts.astype(jnp.int32), axis=1)
    last = jnp.where(count > 0, first + pairs - 1, chunks)
    used = jnp.maximum(order, 0)
    lists = (
        came,
        entry_of // 2,
        entry_of % 2,
        entry_of // 8,
        used // 2,
        jnp.where(order < 0, 2, order % 2),
        used // 8,
        keep,
        last,
    )
    return jnp.concatenate([x.astype(jnp.int32) for x in lists]), chunks


def kernel(
    doms,
    cols,
    classes,
    chunks,
    index,
    features,
    w_hidden,
    w_out,
    values,
    request,
    code,
    prop_out,
    grad_out,
    values_here,
    by_entry,
    by_row,
    tiles,
    head_send,
    stat_send,
    stat_recv,
    want,
    want_s,
    teleports,
    table0,
    table1,
    table2,
    swapped0,
    swapped1,
    swapped2,
    inverse,
    final,
    grad,
    w_plain,
    w_swapped,
    acc,
    come_in,
    remote_tiles,
    local_tiles,
    route,
    out_buf,
    back_buf,
    head_sems,
    stat_sems,
    request_sems,
    local_sem,
    send_sems,
    recv_sems,
):
    me = lax.axis_index("dom")
    my_col = lax.axis_index("col")
    row_blocks = code.shape[0]
    entries = row_blocks * 8
    share = w_out.shape[1] // cols
    mine = features.shape[0] // BLOCK
    slots, spots = doms * CAP, 2 * chunks
    at_slot_tile = entries
    at_slot_half = at_slot_tile + slots
    at_slot_row = at_slot_half + slots
    at_tile = at_slot_row + slots
    at_half = at_tile + spots
    at_row = at_half + spots
    at_keep = at_row + spots
    at_last = at_keep + chunks
    peers = doms - 1
    local_rows = row_blocks * HALF
    table = (table0, table1, table2)
    swapped = (swapped0, swapped1, swapped2)

    lane = lax.broadcasted_iota(jnp.int32, (HALF, LANES), 1)
    low = lane < BLOCK

    def swap(x):
        return pltpu.roll(x, BLOCK, 1)

    def dom_at(shift):
        return lax.rem(me + shift, doms)

    def col_at(shift):
        return lax.rem(my_col + shift, cols)

    to_vmem = pltpu.make_async_copy(values, values_here, local_sem.at[1])
    to_vmem.start()

    barrier = pltpu.get_barrier_semaphore()

    def greet_dom(k, carry):
        pl.semaphore_signal(barrier, inc=1, device_id={"dom": dom_at(k + 1)}, device_id_type=pl.DeviceIdType.MESH)
        return carry

    def greet_col(k, carry):
        pl.semaphore_signal(barrier, inc=1, device_id={"col": col_at(k + 1)}, device_id_type=pl.DeviceIdType.MESH)
        return carry

    lax.fori_loop(0, peers, greet_dom, 0)
    lax.fori_loop(0, cols - 1, greet_col, 0)

    hidden = jax.nn.relu(jnp.dot(features[...], w_hidden[...], preferred_element_type=F32)).astype(BF16)
    heads = jnp.dot(hidden, w_out[...], preferred_element_type=F32).T
    for c in range(cols):
        for pair in range(mine // 2):
            part = heads[c * share : (c + 1) * share, pair * LANES : (pair + 1) * LANES]
            top, bottom = part[:HALF], part[HALF:]
            at = c * mine + pair * 2
            head_send[at] = jnp.where(low, top, swap(bottom)).astype(BF16)
            head_send[at + 1] = jnp.where(low, swap(top), bottom).astype(BF16)

    pl.semaphore_wait(barrier, peers + cols - 1)

    def request_copy(k):
        return pltpu.make_async_remote_copy(
            src_ref=request.at[dom_at(k + 1)],
            dst_ref=want.at[k],
            send_sem=request_sems.at[0],
            recv_sem=request_sems.at[1],
            device_id={"dom": dom_at(k + 1)},
            device_id_type=pl.DeviceIdType.MESH,
        )

    def start_request(k, carry):
        request_copy(k).start()
        return carry

    lax.fori_loop(0, peers, start_request, 0)

    def own(col):
        return pl.ds(col * mine, mine)

    def head_copy(j):
        return pltpu.make_async_remote_copy(
            src_ref=head_send.at[own(col_at(j + 1))],
            dst_ref=teleports.at[own(my_col)],
            send_sem=head_sems.at[0, j],
            recv_sem=head_sems.at[1, j],
            device_id={"col": col_at(j + 1)},
            device_id_type=pl.DeviceIdType.MESH,
        )

    for j in range(cols - 1):
        head_copy(j).start()
    teleports[own(my_col)] = head_send[own(my_col)]

    def row_tiles(r):
        parts = [tiles[4 * r + q] for q in range(4)]
        return jnp.concatenate(parts, axis=1)

    ones = jnp.ones((HALF, 4 * LANES), BF16)
    contract_lanes = (((1,), (1,)), ((), ()))

    def degree(r, carry):
        sums = lax.dot_general(ones, row_tiles(r), contract_lanes, preferred_element_type=F32)
        inverse[r] = 1.0 / (1.0 + jnp.concatenate([sums, sums], axis=1))
        return carry

    def rearrange(group, carry):
        rows = BLOCK * BLOCK // LANES
        first = pl.multiple_of(group * SPREAD, SPREAD)
        for m in range(rows):
            part = values_here[pl.ds(first, SPREAD), m * LANES : (m + 1) * LANES]
            by_entry[pl.ds(m, SPREAD, stride=rows), :] = part.astype(F32)
        left = lax.broadcasted_iota(jnp.int32, (rows, LANES), 1) < BLOCK
        for pair in range(SPREAD // 2):
            one = by_entry[2 * pair * rows : (2 * pair + 1) * rows, :]
            two = by_entry[(2 * pair + 1) * rows : (2 * pair + 2) * rows, :]
            by_row[pl.ds(pair * BLOCK, rows, stride=2), :] = jnp.where(left, one, swap(two))
            by_row[pl.ds(pair * BLOCK + 1, rows, stride=2), :] = jnp.where(left, swap(one), two)
        for pair in range(SPREAD // 2):
            tiles[group * (SPREAD // 2) + pair] = by_row[pair * BLOCK : (pair + 1) * BLOCK, :].astype(BF16)
        return carry

    def all_requests(wait):
        whole = pltpu.make_async_remote_copy(
            src_ref=want.at[pl.ds(0, peers)],
            dst_ref=want.at[pl.ds(0, peers)],
            send_sem=request_sems.at[0],
            recv_sem=request_sems.at[1],
            device_id={"dom": dom_at(1)},
            device_id_type=pl.DeviceIdType.MESH,
        )
        whole.wait_recv() if wait == "recv" else whole.wait_send()

    all_requests("recv")
    want[peers] = jnp.full((1, LANES), row_blocks, jnp.int32)
    teleports[row_blocks] = jnp.zeros((HALF, LANES), BF16)
    w_plain[row_blocks] = jnp.zeros((HALF, LANES), BF16)
    to_scalars = pltpu.make_async_copy(want, want_s, local_sem.at[0])
    to_scalars.start()
    to_scalars.wait()

    for j in range(cols - 1):
        head_copy(j).wait_recv()

    def turn(blocks):
        count = blocks.shape[0]
        flat = swap(blocks.astype(F32).reshape(count * HALF, LANES))
        return flat.astype(BF16).reshape(count, HALF, LANES)

    def swap_first(group, carry):
        at = pl.ds(group * GROUP, GROUP)
        blocks = teleports[at]
        table0[at] = blocks
        swapped[0][at] = turn(blocks)
        return carry

    lax.fori_loop(0, row_blocks // GROUP, swap_first, 0)

    def peer_copy(step, k):
        at = pl.ds(k * CAP, CAP)
        if step < STEPS:
            dst = table[step].at[pl.ds(row_blocks + k * CAP, CAP)]
        else:
            dst = back_buf.at[step - STEPS, at]
        return pltpu.make_async_remote_copy(
            src_ref=out_buf.at[step, at],
            dst_ref=dst,
            send_sem=send_sems.at[step],
            recv_sem=recv_sems.at[step],
            device_id={"dom": dom_at(k + 1)},
            device_id_type=pl.DeviceIdType.MESH,
        )

    def whole_copy(step):
        at = pl.ds(0, peers * CAP)
        dst = table[step].at[pl.ds(row_blocks, peers * CAP)] if step < STEPS else back_buf.at[step - STEPS, at]
        return pltpu.make_async_remote_copy(
            src_ref=out_buf.at[step, at],
            dst_ref=dst,
            send_sem=send_sems.at[step],
            recv_sem=recv_sems.at[step],
            device_id={"dom": dom_at(1)},
            device_id_type=pl.DeviceIdType.MESH,
        )

    def two_blocks(plain, turned, a, b):
        top = jnp.where(low, plain(a), turned(b))
        bottom = jnp.where(low, turned(a), plain(b))
        return jnp.concatenate([top, bottom], axis=0)

    side = jnp.where(lax.broadcasted_iota(jnp.int32, (BLOCK, LANES), 1) < BLOCK, 0, 1)

    def built(start, half):
        pair = tiles[start].astype(F32)
        return jnp.where(side == half, pair, jnp.where(side == 1 - half, swap(pair), 0.0)).astype(BF16)

    def build_tiles(dst, group, at_start, at_side):
        first = group * 4
        made = [built(index[at_start + first + i], index[at_side + first + i]) for i in range(4)]
        at = pl.ds(pl.multiple_of(first * BLOCK, 4 * BLOCK), 4 * BLOCK)
        dst[at, :] = jnp.concatenate(made, axis=0)

    def build_remote(group, carry):
        build_tiles(remote_tiles, group, at_slot_tile, at_slot_half)
        return carry

    def build_local(group, carry):
        build_tiles(local_tiles, group, at_tile, at_half)
        return carry

    def build_route(m, carry):
        row = lax.broadcasted_iota(jnp.int32, (local_rows, LANES), 0)
        col = lax.broadcasted_iota(jnp.int32, (local_rows, LANES), 1)
        wide = lax.broadcasted_iota(jnp.int32, (1, LANES), 1) < BLOCK
        target = jnp.where(wide, want[2 * m], want[2 * m + 1])
        hit = row - col % HALF == target * HALF
        at = pl.ds(pl.multiple_of(m * local_rows, local_rows), local_rows)
        route[at, :] = jnp.where(hit, 1.0, 0.0).astype(BF16)
        return carry

    for step in range(STEPS):
        state_at = teleports if step == 0 else w_plain

        def send(k, carry):
            for c in range(CAP):
                block = want_s[peers - 1 - k, 0, HALF * c]
                out_buf[step, k * CAP + c] = state_at[block]
            peer_copy(step, k).start()
            return carry

        lax.fori_loop(0, peers, send, 0)
        if step == 0:
            to_vmem.wait()
            lax.fori_loop(0, entries // SPREAD, rearrange, 0)
            lax.fori_loop(0, row_blocks, degree, 0, unroll=4)
        elif step == 1:
            lax.fori_loop(0, chunks // 2, build_local, 0)
        else:
            lax.fori_loop(0, peers, build_remote, 0)
            lax.fori_loop(0, doms // 2, build_route, 0)
            acc[chunks] = jnp.zeros((HALF, LANES), F32)
            for late in range(STEPS):
                back_buf[late, pl.ds(peers * CAP, CAP)] = jnp.zeros((CAP, HALF, LANES), BF16)
        whole_copy(step).wait_recv()

        def swap_remote(at):
            swapped[step][at] = turn(table[step][at])

        def swap_group(group, carry):
            swap_remote(pl.ds(row_blocks + group * 2 * GROUP, 2 * GROUP))
            return carry

        whole_groups = peers * CAP // (2 * GROUP)
        lax.fori_loop(0, whole_groups, swap_group, 0)
        swap_remote(pl.ds(row_blocks + whole_groups * 2 * GROUP, peers * CAP - whole_groups * 2 * GROUP))

        def plain(i):
            return table[step][i]

        def turned(i):
            return swapped[step][i]

        def propagate(group, carry):
            rows = [group * GROUP + i for i in range(GROUP)]
            sums = []
            for r in rows:
                picked = [two_blocks(plain, turned, index[8 * r + 2 * q], index[8 * r + 2 * q + 1]) for q in range(4)]
                sums.append(
                    lax.dot_general(
                        jnp.concatenate(picked, axis=1), row_tiles(r), contract_lanes, preferred_element_type=F32
                    )
                )
            sums = jnp.stack([jnp.concatenate([x[:HALF], x[HALF:]], axis=1) for x in sums])
            at = pl.ds(group * GROUP, GROUP)
            rounded, teleport = state_at[at].astype(F32), teleports[at].astype(F32)
            state = (1.0 - TELEPORT) * ((sums + rounded) * inverse[at]) + TELEPORT * teleport
            if step + 1 < STEPS:
                blocks = state.astype(BF16)
                flipped = turn(blocks)
                table[step + 1][at] = blocks
                w_plain[at] = blocks
                swapped[step + 1][at] = flipped
            else:
                final[at] = state
            return carry

        lax.fori_loop(0, row_blocks // GROUP, propagate, 0)

    low_group = lax.broadcasted_iota(jnp.int32, (GROUP, LANES), 1) < BLOCK
    class_id = (
        my_col * share
        + lax.broadcasted_iota(jnp.int32, (HALF, LANES), 0)
        + jnp.where(low, 0, HALF)
    )
    usable = class_id < classes

    def statistics(group, carry):
        at = pl.ds(pl.multiple_of(group * GROUP, GROUP), GROUP)
        state = final[at]
        top = jnp.max(jnp.where(usable, state, FILL), axis=1)
        top = jnp.maximum(top, swap(top))
        expo = jnp.where(usable, jnp.exp(state - top[:, None, :]), 0.0)
        sums = jnp.sum(expo, axis=1)
        sums = sums + swap(sums)
        stat_send[at, :] = jnp.where(low_group, top, sums)
        return carry

    lax.fori_loop(0, row_blocks // GROUP, statistics, 0)

    def stat_copy(j):
        return pltpu.make_async_remote_copy(
            src_ref=stat_send,
            dst_ref=stat_recv.at[j],
            send_sem=stat_sems.at[0, j],
            recv_sem=stat_sems.at[1, j],
            device_id={"col": col_at(j + 1)},
            device_id_type=pl.DeviceIdType.MESH,
        )

    for j in range(cols - 1):
        stat_copy(j).start()

    def unpack(source, dest):
        def pair(m, carry):
            first, second = source[2 * m], source[2 * m + 1]
            at = pl.ds(pl.multiple_of(m * LANES, LANES), LANES)
            dest[pl.ds(0, HALF), at] = jnp.where(low, first, swap(second))
            dest[pl.ds(HALF, HALF), at] = jnp.where(low, swap(first), second)
            return carry

        lax.fori_loop(0, row_blocks // 2, pair, 0, unroll=2)

    unpack(final, prop_out)
    for j in range(cols - 1):
        stat_copy(j).wait_recv()

    wide_low = lax.broadcasted_iota(jnp.int32, (row_blocks, LANES), 1) < BLOCK
    stats = [stat_send[...]] + [stat_recv[j] for j in range(cols - 1)]
    tops = [jnp.where(wide_low, s, swap(s)) for s in stats]
    sums = [jnp.where(wide_low, swap(s), s) for s in stats]
    top = functools.reduce(jnp.maximum, tops)
    whole = functools.reduce(jnp.add, [s * jnp.exp(t - top) for s, t in zip(sums, tops)])
    stat_send_free = [stat_copy(j) for j in range(cols - 1)]
    for copy in stat_send_free:
        copy.wait_send()
    stat_send[...] = top
    stat_recv[0] = 1.0 / whole

    def store_scaled(at, gradient):
        scaled = (inverse[at] * gradient).astype(BF16)
        flipped = turn(scaled)
        w_plain[at] = scaled
        w_swapped[at] = flipped

    def cotangent(group, carry):
        at = pl.ds(pl.multiple_of(group * GROUP, GROUP), GROUP)
        expo = jnp.exp(final[at] - stat_send[at, :][:, None, :])
        probs = expo * stat_recv[0, at, :][:, None, :]
        coded = code[at]
        onehot = jnp.where(class_id == coded % 256, 1.0, 0.0)
        weight = (coded // 256).astype(F32)
        gradient = jnp.where(usable, weight * (probs - onehot), 0.0)
        grad[at] = TELEPORT * gradient
        store_scaled(at, gradient)
        return carry

    lax.fori_loop(0, row_blocks // GROUP, cotangent, 0)

    nothing = jnp.zeros((HALF, LANES), BF16)

    def w_at(i):
        return w_plain[i]

    def w_turned(i):
        return w_swapped[i]

    for late in range(STEPS):

        def products_for(k):
            lines = []
            for c in range(CAP):
                r = index[at_slot_row + CAP * k + c]
                if c % 2 == 0:
                    top, bottom = jnp.where(low, w_at(r), nothing), jnp.where(low, w_turned(r), nothing)
                else:
                    top, bottom = jnp.where(low, nothing, w_turned(r)), jnp.where(low, nothing, w_at(r))
                here = jnp.concatenate([top, bottom], axis=0)
                blank = jnp.zeros_like(here)
                lines.append(jnp.concatenate([here, blank] if c < 2 else [blank, here], axis=1))
            weights = remote_tiles[pl.ds(pl.multiple_of(k * CAP * BLOCK, CAP * BLOCK), CAP * BLOCK), :]
            products = jnp.dot(jnp.concatenate(lines, axis=0), weights, preferred_element_type=F32)
            products = products.reshape(CAP, 2, HALF, LANES)
            return jnp.where(low, products[:, 0], products[:, 1]).astype(BF16)

        def send_back(first, count):
            ready = [products_for(first + i) for i in range(count)]
            for i, blocks in enumerate(ready):
                out_buf[STEPS + late, pl.ds((first + i) * CAP, CAP)] = blocks
            for i in range(count):
                peer_copy(STEPS + late, first + i).start()

        def send_group(group, carry):
            send_back(group * 4, 4)
            return carry

        lax.fori_loop(0, peers // 4, send_group, 0)
        send_back(peers // 4 * 4, peers % 4)

        def local_chunks(group, running):
            terms = []
            for i in range(GROUP):
                m = group * GROUP + i
                a, b = index[at_row + 2 * m], index[at_row + 2 * m + 1]
                weights = local_tiles[pl.ds(pl.multiple_of(m * 2 * BLOCK, 2 * BLOCK), 2 * BLOCK), :]
                products = jnp.dot(two_blocks(w_at, w_turned, a, b), weights, preferred_element_type=F32)
                terms.append(jnp.where(low, products[:HALF], products[HALF:]))
            sums = []
            for i in range(GROUP):
                running = running * index[at_keep + group * GROUP + i].astype(F32) + terms[i]
                sums.append(running)
            acc[pl.ds(group * GROUP, GROUP)] = jnp.stack(sums)
            return running

        lax.fori_loop(0, chunks // GROUP, local_chunks, jnp.zeros((HALF, LANES), F32))

        def local_sum(group, carry):
            picked = [acc[index[at_last + group * GROUP + i]] for i in range(GROUP)]
            come_in[pl.ds(group * GROUP, GROUP)] = jnp.stack(picked)
            return carry

        lax.fori_loop(0, row_blocks // GROUP, local_sum, 0)
        whole_copy(STEPS + late).wait_recv()

        def arrive(m, carry):
            left = route[pl.ds(pl.multiple_of(2 * m * local_rows, local_rows), local_rows), :]
            right = route[pl.ds(pl.multiple_of((2 * m + 1) * local_rows, local_rows), local_rows), :]
            part = back_buf[late, pl.ds(m * 4 * CAP, 4 * CAP)].reshape(4 * PEER, LANES)
            sums = jnp.dot(jnp.concatenate([left, right], axis=1), part, preferred_element_type=F32)
            come_in[...] += sums.reshape(row_blocks, HALF, LANES)
            return carry

        lax.fori_loop(0, doms // 4, arrive, 0)

        def finish(group, carry):
            at = pl.ds(group * GROUP, GROUP)
            gradient = (1.0 - TELEPORT) * (come_in[at] + w_plain[at].astype(F32))
            if late < STEPS - 1:
                grad[at] += TELEPORT * gradient
                store_scaled(at, gradient)
            else:
                grad[at] += gradient
            return carry

        lax.fori_loop(0, row_blocks // GROUP, finish, 0)

    unpack(grad, grad_out)

    all_requests("send")
    for j in range(cols - 1):
        head_copy(j).wait_send()
    for step in range(2 * STEPS):
        whole_copy(step).wait_send()


def body(features, w_hidden, w_out, block_values, block_slot, requested, labels, train_mask):
    doms, cols = lax.axis_size("dom"), lax.axis_size("col")
    nodes = labels.shape[0]
    row_blocks = nodes // BLOCK
    share = w_out.shape[1] // cols
    entries = block_slot.shape[0]
    index, chunks = index_tables(block_slot, doms, row_blocks)
    rows = BLOCK * BLOCK // LANES
    asked = jnp.where(requested < 0, row_blocks, requested)
    request = jnp.broadcast_to(asked.reshape(doms, 1, 1, CAP, 1), (doms, 1, 2, CAP, HALF)).reshape(doms, 1, LANES)
    code = (labels + 256 * train_mask).reshape(row_blocks, 1, 1, BLOCK)
    code = jnp.broadcast_to(code, (row_blocks, 1, 2, BLOCK)).reshape(row_blocks, 1, LANES)
    peers = doms - 1
    local_rows = row_blocks * HALF
    all_blocks = row_blocks + doms * CAP
    vmem, dma = pltpu.VMEM, pltpu.SemaphoreType.DMA
    mine = features.shape[0] // BLOCK
    in_vmem = pl.BlockSpec(memory_space=pltpu.VMEM)
    return pl.pallas_call(
        functools.partial(kernel, doms, cols, NCLASS, chunks),
        out_shape=[jax.ShapeDtypeStruct((share, nodes), F32)] * 2,
        in_specs=[pl.BlockSpec(memory_space=pltpu.SMEM)] + [in_vmem] * 3 + [pl.BlockSpec(memory_space=pl.ANY)] + [in_vmem] * 2,
        out_specs=[in_vmem] * 2,
        scratch_shapes=[
            vmem((entries, BLOCK * BLOCK), BF16),
            vmem((SPREAD * rows, LANES), F32),
            vmem((SPREAD * rows, LANES), F32),
            vmem((entries // 2, BLOCK, LANES), BF16),
            vmem((cols * mine, HALF, LANES), BF16),
            vmem((row_blocks, LANES), F32),
            vmem((cols - 1, row_blocks, LANES), F32),
            vmem((doms, 1, LANES), jnp.int32),
            pltpu.SMEM((doms, 1, LANES), jnp.int32),
            vmem((row_blocks + 1, HALF, LANES), BF16),
            vmem((all_blocks, HALF, LANES), BF16),
            vmem((all_blocks, HALF, LANES), BF16),
            vmem((all_blocks, HALF, LANES), BF16),
            vmem((all_blocks, HALF, LANES), BF16),
            vmem((all_blocks, HALF, LANES), BF16),
            vmem((all_blocks, HALF, LANES), BF16),
            vmem((row_blocks, HALF, LANES), F32),
            vmem((row_blocks, HALF, LANES), F32),
            vmem((row_blocks, HALF, LANES), F32),
            vmem((row_blocks + 1, HALF, LANES), BF16),
            vmem((row_blocks, HALF, LANES), BF16),
            vmem((chunks + 1, HALF, LANES), F32),
            vmem((row_blocks, HALF, LANES), F32),
            vmem((peers * CAP * BLOCK, LANES), BF16),
            vmem((2 * chunks * BLOCK, LANES), BF16),
            vmem((doms // 2 * local_rows, LANES), BF16),
            vmem((2 * STEPS, peers * CAP, HALF, LANES), BF16),
            vmem((STEPS, doms * CAP, HALF, LANES), BF16),
            dma((2, cols - 1)),
            dma((2, cols - 1)),
            dma((2,)),
            dma((2,)),
            dma((2 * STEPS,)),
            dma((2 * STEPS,)),
        ],
        compiler_params=pltpu.CompilerParams(
            collective_id=0, has_side_effects=True, vmem_limit_bytes=48 * 2**20
        ),
    )(index, features, w_hidden, w_out, block_values, request, code)


def solution(mesh):
    return jax.shard_map(
        body,
        mesh=mesh,
        in_specs=(
            P(("dom", "col"), None),
            P(),
            P(),
            P("dom", None),
            P("dom"),
            P("dom", None, None),
            P("dom"),
            P("dom"),
        ),
        out_specs=(P("col", "dom"), P("col", "dom")),
        check_vma=False,
    )
```

```python
import functools
import math

import jax
import jax.numpy as jnp
from jax import lax
from jax.experimental import pallas as pl
from jax.experimental.pallas import tpu as pltpu
from jax.sharding import PartitionSpec as P

NCLASS = 172
BLOCK = 64
STEPS = 3
CAP = 4
TELEPORT = 0.1
FILL = -1e30

HALF = 16
LANES = 128
HALVES = 2
PAIRS = CAP // 2
SPREAD = 32
GROUP = 8

F32 = jnp.float32
BF16 = jnp.bfloat16
MESH = pl.DeviceIdType.MESH


def index_tables(block_slot, doms, row_blocks):
    entries = block_slot.shape[0]
    me = lax.axis_index("dom")
    chunks = -(-((entries - (doms - 1) + row_blocks) // 2) // GROUP) * GROUP
    near = row_blocks // 2 + 1
    far = row_blocks // 2 + (doms - 1) * PAIRS
    entry = jnp.arange(entries, dtype=jnp.int32)
    blocks = jnp.arange(row_blocks, dtype=jnp.int32)
    local = block_slot < row_blocks
    peer = (block_slot - row_blocks) // CAP
    place = (block_slot - row_blocks) % CAP
    came = jnp.where(local, block_slot, row_blocks + ((me - peer - 1) % doms) * CAP + place)
    came = came // 2 + jnp.where(came % 2 == entry % 2, 0, far)
    goes = jnp.where(local, -1, ((peer - me - 1) % doms) * CAP + place)
    slots = jnp.arange(doms * CAP, dtype=jnp.int32)
    entry_of = jnp.sum(jnp.where(goes[None, :] == slots[:, None], entry[None, :], 0), axis=1)
    row_of = entry_of // 8
    count = jnp.sum((block_slot[None, :] == blocks[:, None]).astype(jnp.int32), axis=1)
    pairs = (count + 1) // 2
    first = jnp.sum(jnp.where(blocks[None, :] < blocks[:, None], pairs[None, :], 0), axis=1)
    before = jnp.sum(jnp.where(blocks[None, :] < block_slot[:, None], pairs[None, :], 0), axis=1)
    same = (block_slot[None, :] == block_slot[:, None]) & (entry[None, :] < entry[:, None])
    rank = jnp.sum(same.astype(jnp.int32), axis=1)
    at = jnp.where(local, 2 * before + rank, -1)
    spots = jnp.arange(2 * chunks, dtype=jnp.int32)
    coded = 2 * entry + block_slot % 2 + 1
    order = jnp.sum(jnp.where(at[None, :] == spots[:, None], coded[None, :], 0), axis=1) - 1
    used = jnp.maximum(order, 0) // 2
    row = used // 8
    chunk = jnp.arange(chunks, dtype=jnp.int32)
    starts = (first[None, :] == chunk[:, None]) & (count[None, :] > 0)
    keep = 1 - jnp.max(starts.astype(jnp.int32), axis=1)
    lists = (
        came,
        entry_of // 2,
        slots % 2 + jnp.where(entry_of % 2 == slots % 2, 0, 4),
        row_of // 2 + jnp.where(row_of % 2 == slots % 2, 0, near),
        used // 2,
        jnp.where(order < 0, 2, order % 2 + jnp.where(used % 2 == order % 2, 0, 4)),
        row // 2 + jnp.where(row % 2 == spots % 2, 0, near),
        keep,
        jnp.where(count > 0, first + pairs - 1, chunks),
    )
    return jnp.concatenate([x.astype(jnp.int32) for x in lists]), chunks


def kernel(
    doms,
    cols,
    classes,
    chunks,
    index,
    features,
    w_hidden,
    w_out,
    values,
    request,
    code,
    prop_out,
    grad_out,
    features_here,
    hidden_here,
    out_here,
    values_here,
    by_entry,
    by_row,
    tiles,
    head_send,
    stat_send,
    stat_recv,
    want,
    want_s,
    teleports,
    table00,
    table01,
    table10,
    table11,
    table20,
    table21,
    near0,
    near1,
    inverse,
    final,
    grad,
    acc,
    come_in,
    remote_tiles,
    local_tiles,
    route,
    out_buf,
    back_buf,
    head_sems,
    stat_sems,
    request_sems,
    local_sems,
    send_sems,
    recv_sems,
):
    me = lax.axis_index("dom")
    my_col = lax.axis_index("col")
    row_pairs = code.shape[0]
    row_blocks = 2 * row_pairs
    entries = row_blocks * 8
    share = w_out.shape[1] // cols
    mine = features.shape[0] // LANES
    peers = doms - 1
    slots, spots = doms * CAP, 2 * chunks
    at_slot_tile = entries
    at_slot_side = at_slot_tile + slots
    at_slot_row = at_slot_side + slots
    at_tile = at_slot_row + slots
    at_side = at_tile + spots
    at_row = at_side + spots
    at_keep = at_row + spots
    at_last = at_keep + chunks
    near_pairs = row_pairs + 1
    far_pairs = row_pairs + peers * PAIRS
    pair_group = GROUP // 2
    table = ((table00, table01), (table10, table11), (table20, table21))
    near = (near0, near1)

    low = lax.broadcasted_iota(jnp.int32, (HALF, LANES), 1) < BLOCK

    def swap(x):
        return pltpu.roll(x, BLOCK, 1)

    def turn(blocks):
        count = blocks.shape[0]
        flat = swap(blocks.astype(F32).reshape(count * HALF, LANES))
        return flat.astype(BF16).reshape(count, HALF, LANES)

    def dom_at(shift):
        return lax.rem(me + shift, doms)

    def col_at(shift):
        return lax.rem(my_col + shift, cols)

    stride = 12 if math.gcd(12, peers) == 1 else 1

    def mixed(i):
        return lax.rem(i * stride + peers // 2, peers)

    loads = [
        pltpu.make_async_copy(src, dst, local_sems.at[i])
        for i, (src, dst) in enumerate(
            ((features, features_here), (w_hidden, hidden_here), (w_out, out_here), (values, values_here))
        )
    ]
    for load in loads:
        load.start()

    barrier = pltpu.get_barrier_semaphore()

    def greet_dom(k, carry):
        pl.semaphore_signal(barrier, inc=1, device_id={"dom": dom_at(k + 1)}, device_id_type=MESH)
        return carry

    def greet_col(k, carry):
        pl.semaphore_signal(barrier, inc=1, device_id={"col": col_at(k + 1)}, device_id_type=MESH)
        return carry

    lax.fori_loop(0, peers, greet_dom, 0)
    lax.fori_loop(0, cols - 1, greet_col, 0)

    for load in loads[:3]:
        load.wait()
    hidden = jax.nn.relu(jnp.dot(features_here[...], hidden_here[...], preferred_element_type=F32)).astype(BF16)
    heads = jnp.dot(hidden, out_here[...], preferred_element_type=F32).T.astype(BF16)
    for c in range(cols):
        for pair in range(mine):
            for u in range(HALVES):
                first = c * share + u * HALF
                head_send[c * mine + pair, u] = heads[first : first + HALF, pair * LANES : (pair + 1) * LANES]

    pl.semaphore_wait(barrier, peers + cols - 1)

    def request_copy(k):
        return pltpu.make_async_remote_copy(
            src_ref=request.at[dom_at(k + 1)],
            dst_ref=want.at[k],
            send_sem=request_sems.at[0],
            recv_sem=request_sems.at[1],
            device_id={"dom": dom_at(k + 1)},
            device_id_type=MESH,
        )

    def start_request(k, carry):
        request_copy(k).start()
        return carry

    lax.fori_loop(0, peers, start_request, 0)

    def own(col):
        return pl.ds(col * mine, mine)

    def head_copy(j):
        return pltpu.make_async_remote_copy(
            src_ref=head_send.at[own(col_at(j + 1))],
            dst_ref=teleports.at[own(my_col)],
            send_sem=head_sems.at[0, j],
            recv_sem=head_sems.at[1, j],
            device_id={"col": col_at(j + 1)},
            device_id_type=MESH,
        )

    for j in range(cols - 1):
        head_copy(j).start()
    teleports[own(my_col)] = head_send[own(my_col)]

    def all_requests():
        return pltpu.make_async_remote_copy(
            src_ref=want.at[pl.ds(0, peers)],
            dst_ref=want.at[pl.ds(0, peers)],
            send_sem=request_sems.at[0],
            recv_sem=request_sems.at[1],
            device_id={"dom": dom_at(1)},
            device_id_type=MESH,
        )

    all_requests().wait_recv()
    want[peers] = jnp.full((1, LANES), row_pairs, jnp.int32)
    to_scalars = pltpu.make_async_copy(want, want_s, local_sems.at[4])
    to_scalars.start()
    for u in range(HALVES):
        near[u][row_pairs] = jnp.zeros((HALF, LANES), BF16)
    for j in range(cols - 1):
        head_copy(j).wait_recv()

    def keep_state(step, u, at, later, blocks):
        flipped = turn(blocks)
        near[u][at] = blocks
        near[u][later(near_pairs)] = flipped
        if step is not None:
            table[step][u][at] = blocks
            table[step][u][later(far_pairs)] = flipped

    def places(group):
        return pl.ds(group * pair_group, pair_group), lambda by: pl.ds(by + group * pair_group, pair_group)

    groups = row_pairs // pair_group

    def first_state(group, carry):
        at, later = places(group)
        blocks = teleports[at]
        for u in range(HALVES):
            keep_state(0, u, at, later, blocks[:, u])
        return carry

    lax.fori_loop(0, groups, first_state, 0)
    to_scalars.wait()

    def exchange(step, u, first, count):
        at = pl.ds(first * PAIRS, count * PAIRS)
        if step < STEPS:
            dst = table[step][u].at[pl.ds(row_pairs + first * PAIRS, count * PAIRS)]
        else:
            dst = back_buf.at[step - STEPS, u, at]
        return pltpu.make_async_remote_copy(
            src_ref=out_buf.at[step, u, at],
            dst_ref=dst,
            send_sem=send_sems.at[step, u],
            recv_sem=recv_sems.at[step, u],
            device_id={"dom": dom_at(first + 1)},
            device_id_type=MESH,
        )

    def two(source, a, b):
        return jnp.where(low, source[a], source[b])

    def send_state(step, u):
        def send(i, carry):
            k = mixed(i)
            asked = [want_s[peers - 1 - k, 0, HALF * c] for c in range(CAP)]
            ready = [two(near[u], asked[2 * t], asked[2 * t + 1]) for t in range(PAIRS)]
            out_buf[step, u, pl.ds(k * PAIRS, PAIRS)] = jnp.stack(ready)
            exchange(step, u, k, 1).start()
            return carry

        lax.fori_loop(0, peers, send, 0)

    for u in range(HALVES):
        send_state(0, u)

    loads[3].wait()

    def rearrange(group, carry):
        rows = BLOCK * BLOCK // LANES
        first = pl.multiple_of(group * SPREAD, SPREAD)
        for m in range(rows):
            part = values_here[pl.ds(first, SPREAD), m * LANES : (m + 1) * LANES]
            by_entry[pl.ds(m, SPREAD, stride=rows), :] = part.astype(F32)
        left = lax.broadcasted_iota(jnp.int32, (rows, LANES), 1) < BLOCK
        for pair in range(SPREAD // 2):
            one = by_entry[2 * pair * rows : (2 * pair + 1) * rows, :]
            two_ = by_entry[(2 * pair + 1) * rows : (2 * pair + 2) * rows, :]
            by_row[pl.ds(pair * BLOCK, rows, stride=2), :] = jnp.where(left, one, swap(two_))
            by_row[pl.ds(pair * BLOCK + 1, rows, stride=2), :] = jnp.where(left, swap(one), two_)
        for pair in range(SPREAD // 2):
            tiles[group * (SPREAD // 2) + pair] = by_row[pair * BLOCK : (pair + 1) * BLOCK, :].astype(BF16)
        return carry

    lax.fori_loop(0, entries // SPREAD, rearrange, 0)

    def row_tiles(r):
        return jnp.concatenate([tiles[4 * r + q] for q in range(4)], axis=1)

    contract_lanes = (((1,), (1,)), ((), ()))
    ones = jnp.ones((HALF, 4 * LANES), BF16)

    def row_products(left, r):
        return lax.dot_general(left, row_tiles(r), contract_lanes, preferred_element_type=F32)

    def degree(group, carry):
        sums = [row_products(ones, group * GROUP + i) for i in range(GROUP)]
        sums = jnp.stack([jnp.concatenate(sums[2 * i : 2 * i + 2], axis=1) for i in range(pair_group)])
        inverse[pl.ds(group * pair_group, pair_group)] = 1.0 / (1.0 + sums)
        return carry

    lax.fori_loop(0, groups, degree, 0)

    side_of = jnp.where(lax.broadcasted_iota(jnp.int32, (BLOCK, LANES), 1) < BLOCK, 0, 1)

    def build_tiles(dst, group, at_start, at_code):
        made = []
        for i in range(4):
            pair, coded = tiles[index[at_start + 4 * group + i]].astype(F32), index[at_code + 4 * group + i]
            turned = jnp.where(side_of == coded - 4, swap(pair), 0.0)
            made.append(jnp.where(side_of == coded, pair, turned).astype(BF16))
        at = pl.ds(pl.multiple_of(group * 4 * BLOCK, 4 * BLOCK), 4 * BLOCK)
        dst[at, :] = jnp.concatenate(made, axis=0)

    def build_remote(group, carry):
        build_tiles(remote_tiles, group, at_slot_tile, at_slot_side)
        return carry

    def build_local(group, carry):
        build_tiles(local_tiles, group, at_tile, at_side)
        return carry

    route_rows = 2 * row_pairs * HALF

    def build_route(m, carry):
        row = lax.broadcasted_iota(jnp.int32, (route_rows, LANES), 0)
        col = lax.broadcasted_iota(jnp.int32, (route_rows, LANES), 1)
        wide = lax.broadcasted_iota(jnp.int32, (1, LANES), 1) < BLOCK
        asked = jnp.where(wide, want[2 * m], want[2 * m + 1])
        target = jnp.where(asked < row_pairs, asked, jnp.where(asked == row_pairs, -row_pairs, asked - 1))
        hit = row - col % HALF == target * HALF
        at = pl.ds(pl.multiple_of(m * route_rows, route_rows), route_rows)
        route[at, :] = jnp.where(hit, 1.0, 0.0).astype(BF16)
        return carry

    def show(out, u, group, blocks):
        for i in range(pair_group):
            at = pl.ds(pl.multiple_of((group * pair_group + i) * LANES, LANES), LANES)
            out[u * HALF : (u + 1) * HALF, at] = blocks[i]

    for step in range(STEPS):
        for u in range(HALVES):
            if (step, u) == (1, 0):
                lax.fori_loop(0, chunks // 4, build_local, 0)
            elif (step, u) == (1, 1):
                lax.fori_loop(chunks // 4, chunks // 2, build_local, 0)
            elif (step, u) == (2, 0):
                lax.fori_loop(0, peers, build_remote, 0)
            elif (step, u) == (2, 1):
                lax.fori_loop(0, doms // 2, build_route, 0)
                acc[chunks] = jnp.zeros((HALF, LANES), F32)
                blank = jnp.zeros((PAIRS, HALF, LANES), BF16)
                for late in range(STEPS):
                    for v in range(HALVES):
                        back_buf[late, v, pl.ds(peers * PAIRS, PAIRS)] = blank
            exchange(step, u, 0, peers).wait_recv()
            here = table[step][u]

            def turn_some(first, count):
                here[pl.ds(far_pairs + first, count)] = turn(here[pl.ds(first, count)])

            def turn_group(group, carry):
                turn_some(row_pairs + group * 2 * GROUP, 2 * GROUP)
                return carry

            whole_groups = peers * PAIRS // (2 * GROUP)
            lax.fori_loop(0, whole_groups, turn_group, 0)
            done = whole_groups * 2 * GROUP
            turn_some(row_pairs + done, peers * PAIRS - done)

            def propagate(group, carry):
                sums = []
                for i in range(GROUP):
                    r = group * GROUP + i
                    picked = [two(here, index[8 * r + 2 * q], index[8 * r + 2 * q + 1]) for q in range(4)]
                    sums.append(row_products(jnp.concatenate(picked, axis=1), r))
                sums = jnp.stack([jnp.concatenate(sums[2 * i : 2 * i + 2], axis=1) for i in range(pair_group)])
                at, later = places(group)
                rounded, teleport = near[u][at].astype(F32), teleports[at, u].astype(F32)
                state = (1.0 - TELEPORT) * ((sums + rounded) * inverse[at]) + TELEPORT * teleport
                if step + 1 < STEPS:
                    keep_state(step + 1, u, at, later, state.astype(BF16))
                else:
                    final[u, at] = state
                    show(prop_out, u, group, state)
                return carry

            lax.fori_loop(0, groups, propagate, 0)
            if step + 1 < STEPS:
                send_state(step + 1, u)

    def class_id(u):
        return my_col * share + u * HALF + lax.broadcasted_iota(jnp.int32, (HALF, LANES), 0)

    state = [final[u] for u in range(HALVES)]
    usable = [class_id(u) < classes for u in range(HALVES)]
    top = functools.reduce(
        jnp.maximum, [jnp.max(jnp.where(usable[u], state[u], FILL), axis=1) for u in range(HALVES)]
    )
    sums = functools.reduce(
        jnp.add,
        [
            jnp.sum(jnp.where(usable[u], jnp.exp(state[u] - top[:, None, :]), 0.0), axis=1)
            for u in range(HALVES)
        ],
    )
    stat_send[0] = top
    stat_send[1] = sums

    def stat_copy(j):
        return pltpu.make_async_remote_copy(
            src_ref=stat_send,
            dst_ref=stat_recv.at[j],
            send_sem=stat_sems.at[0, j],
            recv_sem=stat_sems.at[1, j],
            device_id={"col": col_at(j + 1)},
            device_id_type=MESH,
        )

    for j in range(cols - 1):
        stat_copy(j).start()
    for j in range(cols - 1):
        stat_copy(j).wait_recv()
    tops = [stat_send[0]] + [stat_recv[j, 0] for j in range(cols - 1)]
    sums = [stat_send[1]] + [stat_recv[j, 1] for j in range(cols - 1)]
    top = functools.reduce(jnp.maximum, tops)
    whole = functools.reduce(jnp.add, [s * jnp.exp(t - top) for s, t in zip(sums, tops)])
    stat_recv[0, 0] = top
    stat_recv[0, 1] = 1.0 / whole

    def send_products(late, u):
        def products_for(k):
            ready = []
            for t in range(PAIRS):
                slot = at_slot_row + CAP * k + 2 * t
                at = pl.ds(pl.multiple_of((k * PAIRS + t) * LANES, LANES), LANES)
                left = two(near[u], index[slot], index[slot + 1])
                ready.append(jnp.dot(left, remote_tiles[at, :], preferred_element_type=F32))
            return jnp.stack(ready).astype(BF16)

        def send(first, count):
            order = [mixed(first + i) for i in range(count)]
            ready = [products_for(k) for k in order]
            for k, blocks in zip(order, ready):
                out_buf[STEPS + late, u, pl.ds(k * PAIRS, PAIRS)] = blocks
            for k in order:
                exchange(STEPS + late, u, k, 1).start()

        def send_group(group, carry):
            send(group * 4, 4)
            return carry

        lax.fori_loop(0, peers // 4, send_group, 0)
        send(peers // 4 * 4, peers % 4)

    for u in range(HALVES):

        def cotangent(group, carry):
            at, later = places(group)
            rows = pl.ds(group * pair_group, pair_group)
            expo = jnp.exp(final[u, at] - stat_recv[0, 0, rows, :][:, None, :])
            probs = expo * stat_recv[0, 1, rows, :][:, None, :]
            coded = code[at]
            onehot = jnp.where(class_id(u) == coded % 256, 1.0, 0.0)
            weight = (coded // 256).astype(F32)
            gradient = jnp.where(usable[u], weight * (probs - onehot), 0.0)
            grad[u, at] = TELEPORT * gradient
            keep_state(None, u, at, later, (inverse[at] * gradient).astype(BF16))
            return carry

        lax.fori_loop(0, groups, cotangent, 0, unroll=True)
        send_products(0, u)

    for late in range(STEPS):
        for u in range(HALVES):

            def local_chunks(group, running):
                terms = []
                for i in range(GROUP):
                    m = group * GROUP + i
                    left = two(near[u], index[at_row + 2 * m], index[at_row + 2 * m + 1])
                    weights = local_tiles[pl.ds(pl.multiple_of(m * LANES, LANES), LANES), :]
                    terms.append(jnp.dot(left, weights, preferred_element_type=F32))
                sums = []
                for i in range(GROUP):
                    running = running * index[at_keep + group * GROUP + i].astype(F32) + terms[i]
                    sums.append(running)
                acc[pl.ds(group * GROUP, GROUP)] = jnp.stack(sums)
                return running

            lax.fori_loop(0, chunks // GROUP, local_chunks, jnp.zeros((HALF, LANES), F32))

            def local_sum(group, carry):
                picked = [acc[index[at_last + group * GROUP + i]] for i in range(GROUP)]
                come_in[pl.ds(group * pair_group, pair_group)] = jnp.stack(
                    [picked[2 * i] + picked[2 * i + 1] for i in range(pair_group)]
                )
                return carry

            lax.fori_loop(0, groups, local_sum, 0)
            exchange(STEPS + late, u, 0, peers).wait_recv()

            def arrive(m, carry):
                first = [pl.multiple_of((2 * m + i) * route_rows, route_rows) for i in range(2)]
                left = jnp.concatenate([route[pl.ds(f, route_rows), :] for f in first], axis=1)
                part = back_buf[late, u, pl.ds(m * 4 * PAIRS, 4 * PAIRS)]
                none = jnp.zeros_like(part)
                part = jnp.stack([jnp.where(low, part, none), jnp.where(low, none, part)], axis=1)
                sums = jnp.dot(left, part.reshape(4 * CAP * HALF, LANES), preferred_element_type=F32)
                own_half, other = sums[: route_rows // 2], swap(sums[route_rows // 2 :])
                come_in[...] += (own_half + other).reshape(row_pairs, HALF, LANES)
                return carry

            lax.fori_loop(0, doms // 4, arrive, 0)

            def finish(group, carry):
                at, later = places(group)
                gradient = (1.0 - TELEPORT) * (come_in[at] + near[u][at].astype(F32))
                if late < STEPS - 1:
                    grad[u, at] += TELEPORT * gradient
                    keep_state(None, u, at, later, (inverse[at] * gradient).astype(BF16))
                else:
                    show(grad_out, u, group, grad[u, at] + gradient)
                return carry

            lax.fori_loop(0, groups, finish, 0)
            if late < STEPS - 1:
                send_products(late + 1, u)

    all_requests().wait_send()
    for j in range(cols - 1):
        head_copy(j).wait_send()
        stat_copy(j).wait_send()
    for step in range(2 * STEPS):
        for u in range(HALVES):
            exchange(step, u, 0, peers).wait_send()


def body(features, w_hidden, w_out, block_values, block_slot, requested, labels, train_mask):
    doms, cols = lax.axis_size("dom"), lax.axis_size("col")
    nodes = labels.shape[0]
    row_blocks = nodes // BLOCK
    row_pairs = row_blocks // 2
    share = w_out.shape[1] // cols
    entries = block_slot.shape[0]
    index, chunks = index_tables(block_slot, doms, row_blocks)
    side = jnp.arange(CAP, dtype=jnp.int32) % 2
    asked = requested // 2 + jnp.where(requested % 2 == side, 0, row_pairs + 1)
    asked = jnp.where(requested < 0, row_pairs, asked)
    request = jnp.broadcast_to(asked.reshape(doms, 1, 1, CAP, 1), (doms, 1, 2, CAP, HALF)).reshape(doms, 1, LANES)
    code = (labels + 256 * train_mask).reshape(row_pairs, 1, LANES)
    peers = doms - 1
    far_pairs = row_pairs + peers * PAIRS
    rows = BLOCK * BLOCK // LANES
    mine = features.shape[0] // LANES
    vmem, dma = pltpu.VMEM, pltpu.SemaphoreType.DMA
    block = (HALF, LANES)
    in_vmem = pl.BlockSpec(memory_space=pltpu.VMEM)
    anywhere = pl.BlockSpec(memory_space=pl.ANY)
    return pl.pallas_call(
        functools.partial(kernel, doms, cols, NCLASS, chunks),
        out_shape=[jax.ShapeDtypeStruct((share, nodes), F32)] * 2,
        in_specs=[pl.BlockSpec(memory_space=pltpu.SMEM)] + [anywhere] * 4 + [in_vmem] * 2,
        out_specs=[in_vmem] * 2,
        scratch_shapes=[
            vmem(features.shape, BF16),
            vmem(w_hidden.shape, BF16),
            vmem(w_out.shape, BF16),
            vmem((entries, BLOCK * BLOCK), BF16),
            vmem((SPREAD * rows, LANES), F32),
            vmem((SPREAD * rows, LANES), F32),
            vmem((entries // 2, BLOCK, LANES), BF16),
            vmem((cols * mine, HALVES, *block), BF16),
            vmem((2, row_pairs, LANES), F32),
            vmem((cols - 1, 2, row_pairs, LANES), F32),
            vmem((doms, 1, LANES), jnp.int32),
            pltpu.SMEM((doms, 1, LANES), jnp.int32),
            vmem((row_pairs, HALVES, *block), BF16),
            *[vmem((2 * far_pairs, *block), BF16) for _ in range(STEPS * HALVES)],
            *[vmem((2 * (row_pairs + 1), *block), BF16) for _ in range(HALVES)],
            vmem((row_pairs, *block), F32),
            vmem((HALVES, row_pairs, *block), F32),
            vmem((HALVES, row_pairs, *block), F32),
            vmem((chunks + 1, *block), F32),
            vmem((row_pairs, *block), F32),
            vmem((peers * CAP * BLOCK, LANES), BF16),
            vmem((2 * chunks * BLOCK, LANES), BF16),
            vmem((doms // 2 * 2 * row_pairs * HALF, LANES), BF16),
            vmem((2 * STEPS, HALVES, peers * PAIRS, *block), BF16),
            vmem((STEPS, HALVES, doms * PAIRS, *block), BF16),
            dma((2, cols - 1)),
            dma((2, cols - 1)),
            dma((2,)),
            dma((5,)),
            dma((2 * STEPS, HALVES)),
            dma((2 * STEPS, HALVES)),
        ],
        compiler_params=pltpu.CompilerParams(
            collective_id=0, has_side_effects=True, vmem_limit_bytes=48 * 2**20
        ),
    )(index, features, w_hidden, w_out, block_values, request, code)


def solution(mesh):
    return jax.shard_map(
        body,
        mesh=mesh,
        in_specs=(
            P(("dom", "col"), None),
            P(),
            P(),
            P("dom", None),
            P("dom"),
            P("dom", None, None),
            P("dom"),
            P("dom"),
        ),
        out_specs=(P("col", "dom"), P("col", "dom")),
        check_vma=False,
    )
```

```python
import functools
import math

import jax
import jax.numpy as jnp
from jax import lax
from jax.experimental import pallas as pl
from jax.experimental.pallas import tpu as pltpu
from jax.sharding import PartitionSpec as P

NCLASS = 172
BLOCK = 64
STEPS = 3
CAP = 4
TELEPORT = 0.1
FILL = -1e30

HALF = 16
LANES = 128
HALVES = 2
PAIRS = CAP // 2
SPREAD = 32
GROUP = 8

F32 = jnp.float32
BF16 = jnp.bfloat16
MESH = pl.DeviceIdType.MESH


def index_tables(block_slot, doms, row_blocks):
    entries = block_slot.shape[0]
    me = lax.axis_index("dom")
    chunks = -(-((entries - (doms - 1) + row_blocks) // 2) // GROUP) * GROUP
    near = row_blocks // 2 + 1
    far = row_blocks // 2 + (doms - 1) * PAIRS
    entry = jnp.arange(entries, dtype=jnp.int32)
    blocks = jnp.arange(row_blocks, dtype=jnp.int32)
    local = block_slot < row_blocks
    peer = (block_slot - row_blocks) // CAP
    place = (block_slot - row_blocks) % CAP
    came = jnp.where(local, block_slot, row_blocks + ((me - peer - 1) % doms) * CAP + place)
    came = came // 2 + jnp.where(came % 2 == entry % 2, 0, far)
    goes = jnp.where(local, -1, ((peer - me - 1) % doms) * CAP + place)
    slots = jnp.arange(doms * CAP, dtype=jnp.int32)
    entry_of = jnp.sum(jnp.where(goes[None, :] == slots[:, None], entry[None, :], 0), axis=1)
    row_of = entry_of // 8
    count = jnp.sum((block_slot[None, :] == blocks[:, None]).astype(jnp.int32), axis=1)
    pairs = (count + 1) // 2
    first = jnp.sum(jnp.where(blocks[None, :] < blocks[:, None], pairs[None, :], 0), axis=1)
    before = jnp.sum(jnp.where(blocks[None, :] < block_slot[:, None], pairs[None, :], 0), axis=1)
    same = (block_slot[None, :] == block_slot[:, None]) & (entry[None, :] < entry[:, None])
    rank = jnp.sum(same.astype(jnp.int32), axis=1)
    at = jnp.where(local, 2 * before + rank, -1)
    spots = jnp.arange(2 * chunks, dtype=jnp.int32)
    coded = 2 * entry + block_slot % 2 + 1
    order = jnp.sum(jnp.where(at[None, :] == spots[:, None], coded[None, :], 0), axis=1) - 1
    used = jnp.maximum(order, 0) // 2
    row = used // 8
    chunk = jnp.arange(chunks, dtype=jnp.int32)
    starts = (first[None, :] == chunk[:, None]) & (count[None, :] > 0)
    keep = 1 - jnp.max(starts.astype(jnp.int32), axis=1)
    lists = (
        came,
        entry_of // 2,
        slots % 2 + jnp.where(entry_of % 2 == slots % 2, 0, 4),
        row_of // 2 + jnp.where(row_of % 2 == slots % 2, 0, near),
        used // 2,
        jnp.where(order < 0, 2, order % 2 + jnp.where(used % 2 == order % 2, 0, 4)),
        row // 2 + jnp.where(row % 2 == spots % 2, 0, near),
        keep,
        jnp.where(count > 0, first + pairs - 1, chunks),
    )
    return jnp.concatenate([x.astype(jnp.int32) for x in lists]), chunks


def kernel(
    doms,
    cols,
    classes,
    chunks,
    index,
    features,
    w_hidden,
    w_out,
    values,
    request,
    code,
    prop_out,
    grad_out,
    features_here,
    hidden_here,
    out_here,
    values_here,
    by_entry,
    by_row,
    tiles,
    head_send,
    stat_send,
    stat_recv,
    want,
    want_s,
    teleports,
    table00,
    table01,
    table10,
    table11,
    table20,
    table21,
    near0,
    near1,
    inverse,
    final,
    grad,
    acc,
    come_in,
    remote_tiles,
    local_tiles,
    route,
    out_buf,
    back_buf,
    head_sems,
    stat_sems,
    request_sems,
    local_sems,
    send_sems,
    recv_sems,
):
    me = lax.axis_index("dom")
    my_col = lax.axis_index("col")
    row_pairs = code.shape[0]
    row_blocks = 2 * row_pairs
    entries = row_blocks * 8
    share = w_out.shape[1] // cols
    mine = features.shape[0] // LANES
    peers = doms - 1
    slots, spots = doms * CAP, 2 * chunks
    at_slot_tile = entries
    at_slot_side = at_slot_tile + slots
    at_slot_row = at_slot_side + slots
    at_tile = at_slot_row + slots
    at_side = at_tile + spots
    at_row = at_side + spots
    at_keep = at_row + spots
    at_last = at_keep + chunks
    near_pairs = row_pairs + 1
    far_pairs = row_pairs + peers * PAIRS
    pair_group = GROUP // 2
    table = ((table00, table01), (table10, table11), (table20, table21))
    near = (near0, near1)

    low = lax.broadcasted_iota(jnp.int32, (HALF, LANES), 1) < BLOCK

    def swap(x):
        return pltpu.roll(x, BLOCK, 1)

    def turn(blocks):
        count = blocks.shape[0]
        flat = swap(blocks.astype(F32).reshape(count * HALF, LANES))
        return flat.astype(BF16).reshape(count, HALF, LANES)

    def dom_at(shift):
        return lax.rem(me + shift, doms)

    def col_at(shift):
        return lax.rem(my_col + shift, cols)

    stride = 12 if math.gcd(12, peers) == 1 else 1

    def mixed(i):
        return lax.rem(i * stride + peers // 2, peers)

    loads = [
        pltpu.make_async_copy(src, dst, local_sems.at[i])
        for i, (src, dst) in enumerate(
            ((features, features_here), (w_hidden, hidden_here), (w_out, out_here), (values, values_here))
        )
    ]
    for load in loads:
        load.start()

    barrier = pltpu.get_barrier_semaphore()

    def greet_dom(k, carry):
        pl.semaphore_signal(barrier, inc=1, device_id={"dom": dom_at(k + 1)}, device_id_type=MESH)
        return carry

    def greet_col(k, carry):
        pl.semaphore_signal(barrier, inc=1, device_id={"col": col_at(k + 1)}, device_id_type=MESH)
        return carry

    lax.fori_loop(0, peers, greet_dom, 0)
    lax.fori_loop(0, cols - 1, greet_col, 0)

    for load in loads[:3]:
        load.wait()
    hidden = jax.nn.relu(jnp.dot(features_here[...], hidden_here[...], preferred_element_type=F32)).astype(BF16)
    heads = jnp.dot(hidden, out_here[...], preferred_element_type=F32).T.astype(BF16)
    for c in range(cols):
        for pair in range(mine):
            for u in range(HALVES):
                first = c * share + u * HALF
                head_send[c * mine + pair, u] = heads[first : first + HALF, pair * LANES : (pair + 1) * LANES]

    pl.semaphore_wait(barrier, peers + cols - 1)

    def request_copy(k):
        return pltpu.make_async_remote_copy(
            src_ref=request.at[dom_at(k + 1)],
            dst_ref=want.at[k],
            send_sem=request_sems.at[0],
            recv_sem=request_sems.at[1],
            device_id={"dom": dom_at(k + 1)},
            device_id_type=MESH,
        )

    def start_request(k, carry):
        request_copy(k).start()
        return carry

    lax.fori_loop(0, peers, start_request, 0)

    def own(col):
        return pl.ds(col * mine, mine)

    def head_copy(j):
        return pltpu.make_async_remote_copy(
            src_ref=head_send.at[own(col_at(j + 1))],
            dst_ref=teleports.at[own(my_col)],
            send_sem=head_sems.at[0, j],
            recv_sem=head_sems.at[1, j],
            device_id={"col": col_at(j + 1)},
            device_id_type=MESH,
        )

    for j in range(cols - 1):
        head_copy(j).start()
    teleports[own(my_col)] = head_send[own(my_col)]

    def all_requests():
        return pltpu.make_async_remote_copy(
            src_ref=want.at[pl.ds(0, peers)],
            dst_ref=want.at[pl.ds(0, peers)],
            send_sem=request_sems.at[0],
            recv_sem=request_sems.at[1],
            device_id={"dom": dom_at(1)},
            device_id_type=MESH,
        )

    all_requests().wait_recv()
    want[peers] = jnp.full((1, LANES), row_pairs, jnp.int32)
    to_scalars = pltpu.make_async_copy(want, want_s, local_sems.at[4])
    to_scalars.start()
    for u in range(HALVES):
        near[u][row_pairs] = jnp.zeros((HALF, LANES), BF16)
    for j in range(cols - 1):
        head_copy(j).wait_recv()

    def keep_state(step, u, at, later, blocks):
        flipped = turn(blocks)
        near[u][at] = blocks
        near[u][later(near_pairs)] = flipped
        if step is not None:
            table[step][u][at] = blocks
            table[step][u][later(far_pairs)] = flipped

    def places(group):
        return pl.ds(group * pair_group, pair_group), lambda by: pl.ds(by + group * pair_group, pair_group)

    groups = row_pairs // pair_group

    def first_state(group, carry):
        at, later = places(group)
        blocks = teleports[at]
        for u in range(HALVES):
            keep_state(0, u, at, later, blocks[:, u])
        return carry

    lax.fori_loop(0, groups, first_state, 0)
    to_scalars.wait()

    def exchange(step, u, first, count):
        at = pl.ds(first * PAIRS, count * PAIRS)
        if step < STEPS:
            dst = table[step][u].at[pl.ds(row_pairs + first * PAIRS, count * PAIRS)]
        else:
            dst = back_buf.at[step - STEPS, u, at]
        return pltpu.make_async_remote_copy(
            src_ref=out_buf.at[step, u, at],
            dst_ref=dst,
            send_sem=send_sems.at[step, u],
            recv_sem=recv_sems.at[step, u],
            device_id={"dom": dom_at(first + 1)},
            device_id_type=MESH,
        )

    def two(source, a, b):
        return jnp.where(low, source[a], source[b])

    def send_state(step, u):
        def send(i, carry):
            k = mixed(i)
            asked = [want_s[peers - 1 - k, 0, HALF * c] for c in range(CAP)]
            ready = [two(near[u], asked[2 * t], asked[2 * t + 1]) for t in range(PAIRS)]
            out_buf[step, u, pl.ds(k * PAIRS, PAIRS)] = jnp.stack(ready)
            exchange(step, u, k, 1).start()
            return carry

        lax.fori_loop(0, peers, send, 0)

    for u in range(HALVES):
        send_state(0, u)

    loads[3].wait()

    def rearrange(group, carry):
        rows = BLOCK * BLOCK // LANES
        first = pl.multiple_of(group * SPREAD, SPREAD)
        for m in range(rows):
            part = values_here[pl.ds(first, SPREAD), m * LANES : (m + 1) * LANES]
            by_entry[pl.ds(m, SPREAD, stride=rows), :] = part.astype(F32)
        left = lax.broadcasted_iota(jnp.int32, (rows, LANES), 1) < BLOCK
        for pair in range(SPREAD // 2):
            one = by_entry[2 * pair * rows : (2 * pair + 1) * rows, :]
            two_ = by_entry[(2 * pair + 1) * rows : (2 * pair + 2) * rows, :]
            by_row[pl.ds(pair * BLOCK, rows, stride=2), :] = jnp.where(left, one, swap(two_))
            by_row[pl.ds(pair * BLOCK + 1, rows, stride=2), :] = jnp.where(left, swap(one), two_)
        for pair in range(SPREAD // 2):
            tiles[group * (SPREAD // 2) + pair] = by_row[pair * BLOCK : (pair + 1) * BLOCK, :].astype(BF16)
        return carry

    lax.fori_loop(0, entries // SPREAD, rearrange, 0)

    def row_tiles(r):
        return jnp.concatenate([tiles[4 * r + q] for q in range(4)], axis=1)

    contract_lanes = (((1,), (1,)), ((), ()))
    ones = jnp.ones((HALF, 4 * LANES), BF16)

    def row_products(left, r):
        return lax.dot_general(left, row_tiles(r), contract_lanes, preferred_element_type=F32)

    def degree(group, carry):
        sums = [row_products(ones, group * GROUP + i) for i in range(GROUP)]
        sums = jnp.stack([jnp.concatenate(sums[2 * i : 2 * i + 2], axis=1) for i in range(pair_group)])
        inverse[pl.ds(group * pair_group, pair_group)] = 1.0 / (1.0 + sums)
        return carry

    lax.fori_loop(0, groups, degree, 0)

    side_of = jnp.where(lax.broadcasted_iota(jnp.int32, (BLOCK, LANES), 1) < BLOCK, 0, 1)

    def build_tiles(dst, group, at_start, at_code):
        made = []
        for i in range(4):
            pair, coded = tiles[index[at_start + 4 * group + i]].astype(F32), index[at_code + 4 * group + i]
            turned = jnp.where(side_of == coded - 4, swap(pair), 0.0)
            made.append(jnp.where(side_of == coded, pair, turned).astype(BF16))
        at = pl.ds(pl.multiple_of(group * 4 * BLOCK, 4 * BLOCK), 4 * BLOCK)
        dst[at, :] = jnp.concatenate(made, axis=0)

    def build_remote(group, carry):
        build_tiles(remote_tiles, group, at_slot_tile, at_slot_side)
        return carry

    def build_local(group, carry):
        build_tiles(local_tiles, group, at_tile, at_side)
        return carry

    route_rows = row_pairs * HALF

    def build_route(m, carry):
        row = lax.broadcasted_iota(jnp.int32, (route_rows, LANES), 0)
        col = lax.broadcasted_iota(jnp.int32, (route_rows, LANES), 1)
        wide = lax.broadcasted_iota(jnp.int32, (1, LANES), 1) < BLOCK
        asked = jnp.where(wide, want[2 * m], want[2 * m + 1])
        target = jnp.where(asked < row_pairs, asked, jnp.where(asked == row_pairs, -row_pairs, asked - near_pairs))
        hit = row - col % HALF == target * HALF
        at = pl.ds(pl.multiple_of(m * route_rows, route_rows), route_rows)
        route[at, :] = jnp.where(hit, 1.0, 0.0).astype(BF16)
        return carry

    def show(out, u, group, blocks):
        for i in range(pair_group):
            at = pl.ds(pl.multiple_of((group * pair_group + i) * LANES, LANES), LANES)
            out[u * HALF : (u + 1) * HALF, at] = blocks[i]

    for step in range(STEPS):
        for u in range(HALVES):
            if (step, u) == (1, 0):
                lax.fori_loop(0, chunks // 4, build_local, 0)
            elif (step, u) == (1, 1):
                lax.fori_loop(chunks // 4, chunks // 2, build_local, 0)
            elif (step, u) == (2, 0):
                lax.fori_loop(0, peers, build_remote, 0)
            elif (step, u) == (2, 1):
                lax.fori_loop(0, doms // 2, build_route, 0)
                acc[chunks] = jnp.zeros((HALF, LANES), F32)
                blank = jnp.zeros((PAIRS, HALF, LANES), BF16)
                for late in range(STEPS):
                    for v in range(HALVES):
                        back_buf[late, v, pl.ds(peers * PAIRS, PAIRS)] = blank
            exchange(step, u, 0, peers).wait_recv()
            here = table[step][u]

            def turn_some(first, count):
                here[pl.ds(far_pairs + first, count)] = turn(here[pl.ds(first, count)])

            def turn_group(group, carry):
                turn_some(row_pairs + group * 2 * GROUP, 2 * GROUP)
                return carry

            whole_groups = peers * PAIRS // (2 * GROUP)
            lax.fori_loop(0, whole_groups, turn_group, 0)
            done = whole_groups * 2 * GROUP
            turn_some(row_pairs + done, peers * PAIRS - done)

            def propagate(group, carry):
                sums = []
                for i in range(GROUP):
                    r = group * GROUP + i
                    picked = [two(here, index[8 * r + 2 * q], index[8 * r + 2 * q + 1]) for q in range(4)]
                    sums.append(row_products(jnp.concatenate(picked, axis=1), r))
                sums = jnp.stack([jnp.concatenate(sums[2 * i : 2 * i + 2], axis=1) for i in range(pair_group)])
                at, later = places(group)
                rounded, teleport = near[u][at].astype(F32), teleports[at, u].astype(F32)
                state = (1.0 - TELEPORT) * ((sums + rounded) * inverse[at]) + TELEPORT * teleport
                if step + 1 < STEPS:
                    keep_state(step + 1, u, at, later, state.astype(BF16))
                else:
                    final[u, at] = state
                    show(prop_out, u, group, state)
                return carry

            lax.fori_loop(0, groups, propagate, 0)
            if step + 1 < STEPS:
                send_state(step + 1, u)

    def class_id(u):
        return my_col * share + u * HALF + lax.broadcasted_iota(jnp.int32, (HALF, LANES), 0)

    state = [final[u] for u in range(HALVES)]
    usable = [class_id(u) < classes for u in range(HALVES)]
    top = functools.reduce(
        jnp.maximum, [jnp.max(jnp.where(usable[u], state[u], FILL), axis=1) for u in range(HALVES)]
    )
    sums = functools.reduce(
        jnp.add,
        [
            jnp.sum(jnp.where(usable[u], jnp.exp(state[u] - top[:, None, :]), 0.0), axis=1)
            for u in range(HALVES)
        ],
    )
    stat_send[0] = top
    stat_send[1] = sums

    def stat_copy(j):
        return pltpu.make_async_remote_copy(
            src_ref=stat_send,
            dst_ref=stat_recv.at[j],
            send_sem=stat_sems.at[0, j],
            recv_sem=stat_sems.at[1, j],
            device_id={"col": col_at(j + 1)},
            device_id_type=MESH,
        )

    for j in range(cols - 1):
        stat_copy(j).start()
    for j in range(cols - 1):
        stat_copy(j).wait_recv()
    tops = [stat_send[0]] + [stat_recv[j, 0] for j in range(cols - 1)]
    sums = [stat_send[1]] + [stat_recv[j, 1] for j in range(cols - 1)]
    top = functools.reduce(jnp.maximum, tops)
    whole = functools.reduce(jnp.add, [s * jnp.exp(t - top) for s, t in zip(sums, tops)])
    stat_recv[0, 0] = top
    stat_recv[0, 1] = 1.0 / whole

    def send_products(late, u):
        def products_for(k):
            ready = []
            for t in range(PAIRS):
                slot = at_slot_row + CAP * k + 2 * t
                at = pl.ds(pl.multiple_of((k * PAIRS + t) * LANES, LANES), LANES)
                left = two(near[u], index[slot], index[slot + 1])
                ready.append(jnp.dot(left, remote_tiles[at, :], preferred_element_type=F32))
            return jnp.stack(ready).astype(BF16)

        def send(first, count):
            order = [mixed(first + i) for i in range(count)]
            ready = [products_for(k) for k in order]
            for k, blocks in zip(order, ready):
                out_buf[STEPS + late, u, pl.ds(k * PAIRS, PAIRS)] = blocks
            for k in order:
                exchange(STEPS + late, u, k, 1).start()

        def send_group(group, carry):
            send(group * 4, 4)
            return carry

        lax.fori_loop(0, peers // 4, send_group, 0)
        send(peers // 4 * 4, peers % 4)

    for u in range(HALVES):

        def cotangent(group, carry):
            at, later = places(group)
            rows = pl.ds(group * pair_group, pair_group)
            expo = jnp.exp(final[u, at] - stat_recv[0, 0, rows, :][:, None, :])
            probs = expo * stat_recv[0, 1, rows, :][:, None, :]
            coded = code[at]
            onehot = jnp.where(class_id(u) == coded % 256, 1.0, 0.0)
            weight = (coded // 256).astype(F32)
            gradient = jnp.where(usable[u], weight * (probs - onehot), 0.0)
            grad[u, at] = TELEPORT * gradient
            keep_state(None, u, at, later, (inverse[at] * gradient).astype(BF16))
            return carry

        lax.fori_loop(0, groups, cotangent, 0, unroll=True)
        send_products(0, u)

    nothing = jnp.zeros((HALF, LANES), BF16)
    half_of = jnp.where(low, 0, 1)

    for late in range(STEPS):
        for u in range(HALVES):

            def local_chunks(group, running):
                terms = []
                for i in range(GROUP):
                    m = group * GROUP + i
                    left = two(near[u], index[at_row + 2 * m], index[at_row + 2 * m + 1])
                    weights = local_tiles[pl.ds(pl.multiple_of(m * LANES, LANES), LANES), :]
                    terms.append(jnp.dot(left, weights, preferred_element_type=F32))
                sums = []
                for i in range(GROUP):
                    running = running * index[at_keep + group * GROUP + i].astype(F32) + terms[i]
                    sums.append(running)
                acc[pl.ds(group * GROUP, GROUP)] = jnp.stack(sums)
                return running

            lax.fori_loop(0, chunks // GROUP, local_chunks, jnp.zeros((HALF, LANES), F32))

            def local_sum(group, carry):
                picked = [acc[index[at_last + group * GROUP + i]] for i in range(GROUP)]
                come_in[pl.ds(group * pair_group, pair_group)] = jnp.stack(
                    [picked[2 * i] + picked[2 * i + 1] for i in range(pair_group)]
                )
                return carry

            lax.fori_loop(0, groups, local_sum, 0)
            exchange(STEPS + late, u, 0, peers).wait_recv()

            def arrive(m, carry):
                first = [pl.multiple_of((2 * m + i) * route_rows, route_rows) for i in range(2)]
                left = jnp.concatenate([route[pl.ds(f, route_rows), :] for f in first], axis=1)
                part = back_buf[late, u, pl.ds(m * 4 * PAIRS, 4 * PAIRS)]
                flipped = turn(part)
                both = jnp.where(low, part, flipped), jnp.where(low, flipped, part)
                rows = []
                for i in range(4 * CAP):
                    asked = want_s[4 * m + i // CAP, 0, HALF * (i % CAP)]
                    goal = jnp.where(asked < near_pairs, i % 2, 1 - i % 2)
                    rows.append(jnp.where(half_of == goal, both[i % 2][i // 2], nothing))
                sums = jnp.dot(left, jnp.concatenate(rows, axis=0), preferred_element_type=F32)
                come_in[...] += sums.reshape(row_pairs, HALF, LANES)
                return carry

            lax.fori_loop(0, doms // 4, arrive, 0)

            def finish(group, carry):
                at, later = places(group)
                gradient = (1.0 - TELEPORT) * (come_in[at] + near[u][at].astype(F32))
                if late < STEPS - 1:
                    grad[u, at] += TELEPORT * gradient
                    keep_state(None, u, at, later, (inverse[at] * gradient).astype(BF16))
                else:
                    show(grad_out, u, group, grad[u, at] + gradient)
                return carry

            lax.fori_loop(0, groups, finish, 0)
            if late < STEPS - 1:
                send_products(late + 1, u)

    all_requests().wait_send()
    for j in range(cols - 1):
        head_copy(j).wait_send()
        stat_copy(j).wait_send()
    for step in range(2 * STEPS):
        for u in range(HALVES):
            exchange(step, u, 0, peers).wait_send()


def body(features, w_hidden, w_out, block_values, block_slot, requested, labels, train_mask):
    doms, cols = lax.axis_size("dom"), lax.axis_size("col")
    nodes = labels.shape[0]
    row_blocks = nodes // BLOCK
    row_pairs = row_blocks // 2
    share = w_out.shape[1] // cols
    entries = block_slot.shape[0]
    index, chunks = index_tables(block_slot, doms, row_blocks)
    side = jnp.arange(CAP, dtype=jnp.int32) % 2
    asked = requested // 2 + jnp.where(requested % 2 == side, 0, row_pairs + 1)
    asked = jnp.where(requested < 0, row_pairs, asked)
    request = jnp.broadcast_to(asked.reshape(doms, 1, 1, CAP, 1), (doms, 1, 2, CAP, HALF)).reshape(doms, 1, LANES)
    code = (labels + 256 * train_mask).reshape(row_pairs, 1, LANES)
    peers = doms - 1
    far_pairs = row_pairs + peers * PAIRS
    rows = BLOCK * BLOCK // LANES
    mine = features.shape[0] // LANES
    vmem, dma = pltpu.VMEM, pltpu.SemaphoreType.DMA
    block = (HALF, LANES)
    in_vmem = pl.BlockSpec(memory_space=pltpu.VMEM)
    anywhere = pl.BlockSpec(memory_space=pl.ANY)
    return pl.pallas_call(
        functools.partial(kernel, doms, cols, NCLASS, chunks),
        out_shape=[jax.ShapeDtypeStruct((share, nodes), F32)] * 2,
        in_specs=[pl.BlockSpec(memory_space=pltpu.SMEM)] + [anywhere] * 4 + [in_vmem] * 2,
        out_specs=[in_vmem] * 2,
        scratch_shapes=[
            vmem(features.shape, BF16),
            vmem(w_hidden.shape, BF16),
            vmem(w_out.shape, BF16),
            vmem((entries, BLOCK * BLOCK), BF16),
            vmem((SPREAD * rows, LANES), F32),
            vmem((SPREAD * rows, LANES), F32),
            vmem((entries // 2, BLOCK, LANES), BF16),
            vmem((cols * mine, HALVES, *block), BF16),
            vmem((2, row_pairs, LANES), F32),
            vmem((cols - 1, 2, row_pairs, LANES), F32),
            vmem((doms, 1, LANES), jnp.int32),
            pltpu.SMEM((doms, 1, LANES), jnp.int32),
            vmem((row_pairs, HALVES, *block), BF16),
            *[vmem((2 * far_pairs, *block), BF16) for _ in range(STEPS * HALVES)],
            *[vmem((2 * (row_pairs + 1), *block), BF16) for _ in range(HALVES)],
            vmem((row_pairs, *block), F32),
            vmem((HALVES, row_pairs, *block), F32),
            vmem((HALVES, row_pairs, *block), F32),
            vmem((chunks + 1, *block), F32),
            vmem((row_pairs, *block), F32),
            vmem((peers * CAP * BLOCK, LANES), BF16),
            vmem((2 * chunks * BLOCK, LANES), BF16),
            vmem((doms // 2 * row_pairs * HALF, LANES), BF16),
            vmem((2 * STEPS, HALVES, peers * PAIRS, *block), BF16),
            vmem((STEPS, HALVES, doms * PAIRS, *block), BF16),
            dma((2, cols - 1)),
            dma((2, cols - 1)),
            dma((2,)),
            dma((5,)),
            dma((2 * STEPS, HALVES)),
            dma((2 * STEPS, HALVES)),
        ],
        compiler_params=pltpu.CompilerParams(
            collective_id=0, has_side_effects=True, vmem_limit_bytes=48 * 2**20
        ),
    )(index, features, w_hidden, w_out, block_values, request, code)


def solution(mesh):
    return jax.shard_map(
        body,
        mesh=mesh,
        in_specs=(
            P(("dom", "col"), None),
            P(),
            P(),
            P("dom", None),
            P("dom"),
            P("dom", None, None),
            P("dom"),
            P("dom"),
        ),
        out_specs=(P("col", "dom"), P("col", "dom")),
        check_vma=False,
    )
```

```python
import functools
import math

import jax
import jax.numpy as jnp
from jax import lax
from jax.experimental import pallas as pl
from jax.experimental.pallas import tpu as pltpu
from jax.sharding import PartitionSpec as P

NCLASS = 172
BLOCK = 64
STEPS = 3
CAP = 4
TELEPORT = 0.1
FILL = -1e30

HALF = 16
LANES = 128
HALVES = 2
PAIRS = CAP // 2
SPREAD = 32
GROUP = 8

F32 = jnp.float32
BF16 = jnp.bfloat16
MESH = pl.DeviceIdType.MESH


def index_tables(block_slot, doms, row_blocks):
    entries = block_slot.shape[0]
    me = lax.axis_index("dom")
    chunks = -(-((entries - (doms - 1) + row_blocks) // 2) // GROUP) * GROUP
    near = row_blocks // 2 + 1
    far = row_blocks // 2 + (doms - 1) * PAIRS
    entry = jnp.arange(entries, dtype=jnp.int32)
    blocks = jnp.arange(row_blocks, dtype=jnp.int32)
    local = block_slot < row_blocks
    peer = (block_slot - row_blocks) // CAP
    place = (block_slot - row_blocks) % CAP
    came = jnp.where(local, block_slot, row_blocks + ((me - peer - 1) % doms) * CAP + place)
    came = came // 2 + jnp.where(came % 2 == entry % 2, 0, far)
    goes = jnp.where(local, -1, ((peer - me - 1) % doms) * CAP + place)
    slots = jnp.arange(doms * CAP, dtype=jnp.int32)
    entry_of = jnp.sum(jnp.where(goes[None, :] == slots[:, None], entry[None, :], 0), axis=1)
    row_of = entry_of // 8
    count = jnp.sum((block_slot[None, :] == blocks[:, None]).astype(jnp.int32), axis=1)
    pairs = (count + 1) // 2
    first = jnp.sum(jnp.where(blocks[None, :] < blocks[:, None], pairs[None, :], 0), axis=1)
    before = jnp.sum(jnp.where(blocks[None, :] < block_slot[:, None], pairs[None, :], 0), axis=1)
    same = (block_slot[None, :] == block_slot[:, None]) & (entry[None, :] < entry[:, None])
    rank = jnp.sum(same.astype(jnp.int32), axis=1)
    at = jnp.where(local, 2 * before + rank, -1)
    spots = jnp.arange(2 * chunks, dtype=jnp.int32)
    coded = 2 * entry + block_slot % 2 + 1
    order = jnp.sum(jnp.where(at[None, :] == spots[:, None], coded[None, :], 0), axis=1) - 1
    used = jnp.maximum(order, 0) // 2
    row = used // 8
    chunk = jnp.arange(chunks, dtype=jnp.int32)
    starts = (first[None, :] == chunk[:, None]) & (count[None, :] > 0)
    keep = 1 - jnp.max(starts.astype(jnp.int32), axis=1)
    lists = (
        came,
        entry_of // 2,
        slots % 2 + jnp.where(entry_of % 2 == slots % 2, 0, 4),
        row_of // 2 + jnp.where(row_of % 2 == slots % 2, 0, near),
        used // 2,
        jnp.where(order < 0, 2, order % 2 + jnp.where(used % 2 == order % 2, 0, 4)),
        row // 2 + jnp.where(row % 2 == spots % 2, 0, near),
        keep,
        jnp.where(count > 0, first + pairs - 1, chunks),
    )
    return jnp.concatenate([x.astype(jnp.int32) for x in lists]), chunks


def kernel(
    doms,
    cols,
    classes,
    chunks,
    index,
    features,
    w_hidden,
    w_out,
    values,
    request,
    code,
    prop_out,
    grad_out,
    features_here,
    hidden_here,
    out_here,
    values_here,
    by_entry,
    by_row,
    tiles,
    head_send,
    stat_send,
    stat_recv,
    want,
    want_s,
    teleports,
    table00,
    table01,
    table10,
    table11,
    table20,
    table21,
    near0,
    near1,
    inverse,
    final,
    grad,
    acc,
    come_in,
    remote_tiles,
    local_tiles,
    route,
    out_buf,
    back_buf,
    head_sems,
    stat_sems,
    request_sems,
    local_sems,
    send_sems,
    recv_sems,
):
    me = lax.axis_index("dom")
    my_col = lax.axis_index("col")
    row_pairs = code.shape[0]
    row_blocks = 2 * row_pairs
    entries = row_blocks * 8
    share = w_out.shape[1] // cols
    mine = features.shape[0] // LANES
    peers = doms - 1
    slots, spots = doms * CAP, 2 * chunks
    at_slot_tile = entries
    at_slot_side = at_slot_tile + slots
    at_slot_row = at_slot_side + slots
    at_tile = at_slot_row + slots
    at_side = at_tile + spots
    at_row = at_side + spots
    at_keep = at_row + spots
    at_last = at_keep + chunks
    near_pairs = row_pairs + 1
    far_pairs = row_pairs + peers * PAIRS
    pair_group = GROUP // 2
    table = ((table00, table01), (table10, table11), (table20, table21))
    near = (near0, near1)

    low = lax.broadcasted_iota(jnp.int32, (HALF, LANES), 1) < BLOCK

    def swap(x):
        return pltpu.roll(x, BLOCK, 1)

    def turn(blocks):
        count = blocks.shape[0]
        flat = swap(blocks.astype(F32).reshape(count * HALF, LANES))
        return flat.astype(BF16).reshape(count, HALF, LANES)

    def dom_at(shift):
        return lax.rem(me + shift, doms)

    def col_at(shift):
        return lax.rem(my_col + shift, cols)

    stride = 12 if math.gcd(12, peers) == 1 else 1

    def mixed(i):
        return lax.rem(i * stride + peers // 2, peers)

    loads = [
        pltpu.make_async_copy(src, dst, local_sems.at[i])
        for i, (src, dst) in enumerate(
            ((features, features_here), (w_hidden, hidden_here), (w_out, out_here), (values, values_here))
        )
    ]
    for load in loads:
        load.start()

    barrier = pltpu.get_barrier_semaphore()

    def greet_dom(k, carry):
        pl.semaphore_signal(barrier, inc=1, device_id={"dom": dom_at(k + 1)}, device_id_type=MESH)
        return carry

    def greet_col(k, carry):
        pl.semaphore_signal(barrier, inc=1, device_id={"col": col_at(k + 1)}, device_id_type=MESH)
        return carry

    lax.fori_loop(0, peers, greet_dom, 0)
    lax.fori_loop(0, cols - 1, greet_col, 0)

    for load in loads[:3]:
        load.wait()
    hidden = jax.nn.relu(jnp.dot(features_here[...], hidden_here[...], preferred_element_type=F32)).astype(BF16)
    heads = jnp.dot(hidden, out_here[...], preferred_element_type=F32).T.astype(BF16)
    for c in range(cols):
        for pair in range(mine):
            for u in range(HALVES):
                first = c * share + u * HALF
                head_send[c * mine + pair, u] = heads[first : first + HALF, pair * LANES : (pair + 1) * LANES]

    pl.semaphore_wait(barrier, peers + cols - 1)

    def request_copy(k):
        return pltpu.make_async_remote_copy(
            src_ref=request.at[dom_at(k + 1)],
            dst_ref=want.at[k],
            send_sem=request_sems.at[0],
            recv_sem=request_sems.at[1],
            device_id={"dom": dom_at(k + 1)},
            device_id_type=MESH,
        )

    def start_request(k, carry):
        request_copy(k).start()
        return carry

    lax.fori_loop(0, peers, start_request, 0)

    def own(col):
        return pl.ds(col * mine, mine)

    def head_copy(j):
        return pltpu.make_async_remote_copy(
            src_ref=head_send.at[own(col_at(j + 1))],
            dst_ref=teleports.at[own(my_col)],
            send_sem=head_sems.at[0, j],
            recv_sem=head_sems.at[1, j],
            device_id={"col": col_at(j + 1)},
            device_id_type=MESH,
        )

    for j in range(cols - 1):
        head_copy(j).start()
    teleports[own(my_col)] = head_send[own(my_col)]

    def all_requests():
        return pltpu.make_async_remote_copy(
            src_ref=want.at[pl.ds(0, peers)],
            dst_ref=want.at[pl.ds(0, peers)],
            send_sem=request_sems.at[0],
            recv_sem=request_sems.at[1],
            device_id={"dom": dom_at(1)},
            device_id_type=MESH,
        )

    all_requests().wait_recv()
    want[peers] = jnp.full((1, LANES), row_pairs, jnp.int32)
    to_scalars = pltpu.make_async_copy(want, want_s, local_sems.at[4])
    to_scalars.start()
    for u in range(HALVES):
        near[u][row_pairs] = jnp.zeros((HALF, LANES), BF16)
    for j in range(cols - 1):
        head_copy(j).wait_recv()

    def keep_state(step, u, at, later, blocks):
        flipped = turn(blocks)
        near[u][at] = blocks
        near[u][later(near_pairs)] = flipped
        if step is not None:
            table[step][u][at] = blocks
            table[step][u][later(far_pairs)] = flipped

    def places(group):
        return pl.ds(group * pair_group, pair_group), lambda by: pl.ds(by + group * pair_group, pair_group)

    groups = row_pairs // pair_group

    def first_state(group, carry):
        at, later = places(group)
        blocks = teleports[at]
        for u in range(HALVES):
            keep_state(0, u, at, later, blocks[:, u])
        return carry

    lax.fori_loop(0, groups, first_state, 0)
    to_scalars.wait()

    def exchange(step, u, first, count):
        at = pl.ds(first * PAIRS, count * PAIRS)
        if step < STEPS:
            dst = table[step][u].at[pl.ds(row_pairs + first * PAIRS, count * PAIRS)]
        else:
            dst = back_buf.at[step - STEPS, u, at]
        return pltpu.make_async_remote_copy(
            src_ref=out_buf.at[step, u, at],
            dst_ref=dst,
            send_sem=send_sems.at[step, u],
            recv_sem=recv_sems.at[step, u],
            device_id={"dom": dom_at(first + 1)},
            device_id_type=MESH,
        )

    def two(source, a, b):
        return jnp.where(low, source[a], source[b])

    def in_groups(send):
        def send_group(group, carry):
            send(group * GROUP, GROUP)
            return carry

        lax.fori_loop(0, peers // GROUP, send_group, 0)
        send(peers // GROUP * GROUP, peers % GROUP)

    def send_all(step, u, blocks_for):
        def send(first, count):
            order = [mixed(first + i) for i in range(count)]
            ready = [blocks_for(k) for k in order]
            for k, blocks in zip(order, ready):
                out_buf[step, u, pl.ds(k * PAIRS, PAIRS)] = blocks
                exchange(step, u, k, 1).start()

        in_groups(send)

    def send_state(step, u):
        def blocks_for(k):
            asked = [want_s[peers - 1 - k, 0, HALF * c] for c in range(CAP)]
            return jnp.stack([two(near[u], asked[2 * t], asked[2 * t + 1]) for t in range(PAIRS)])

        send_all(step, u, blocks_for)

    for u in range(HALVES):
        send_state(0, u)

    loads[3].wait()

    def rearrange(group, carry):
        rows = BLOCK * BLOCK // LANES
        first = pl.multiple_of(group * SPREAD, SPREAD)
        for m in range(rows):
            part = values_here[pl.ds(first, SPREAD), m * LANES : (m + 1) * LANES]
            by_entry[pl.ds(m, SPREAD, stride=rows), :] = part.astype(F32)
        left = lax.broadcasted_iota(jnp.int32, (rows, LANES), 1) < BLOCK
        for pair in range(SPREAD // 2):
            one = by_entry[2 * pair * rows : (2 * pair + 1) * rows, :]
            two_ = by_entry[(2 * pair + 1) * rows : (2 * pair + 2) * rows, :]
            by_row[pl.ds(pair * BLOCK, rows, stride=2), :] = jnp.where(left, one, swap(two_))
            by_row[pl.ds(pair * BLOCK + 1, rows, stride=2), :] = jnp.where(left, swap(one), two_)
        for pair in range(SPREAD // 2):
            tiles[group * (SPREAD // 2) + pair] = by_row[pair * BLOCK : (pair + 1) * BLOCK, :].astype(BF16)
        return carry

    lax.fori_loop(0, entries // SPREAD, rearrange, 0)

    def row_tiles(r):
        return jnp.concatenate([tiles[4 * r + q] for q in range(4)], axis=1)

    contract_lanes = (((1,), (1,)), ((), ()))
    ones = jnp.ones((HALF, 4 * LANES), BF16)

    def row_products(left, r):
        return lax.dot_general(left, row_tiles(r), contract_lanes, preferred_element_type=F32)

    def degree(group, carry):
        sums = [row_products(ones, group * GROUP + i) for i in range(GROUP)]
        sums = jnp.stack([jnp.concatenate(sums[2 * i : 2 * i + 2], axis=1) for i in range(pair_group)])
        inverse[pl.ds(group * pair_group, pair_group)] = 1.0 / (1.0 + sums)
        return carry

    lax.fori_loop(0, groups, degree, 0)

    side_of = jnp.where(lax.broadcasted_iota(jnp.int32, (BLOCK, LANES), 1) < BLOCK, 0, 1)

    def build_tiles(dst, group, at_start, at_code):
        made = []
        for i in range(4):
            pair, coded = tiles[index[at_start + 4 * group + i]].astype(F32), index[at_code + 4 * group + i]
            turned = jnp.where(side_of == coded - 4, swap(pair), 0.0)
            made.append(jnp.where(side_of == coded, pair, turned).astype(BF16))
        at = pl.ds(pl.multiple_of(group * 4 * BLOCK, 4 * BLOCK), 4 * BLOCK)
        dst[at, :] = jnp.concatenate(made, axis=0)

    def build_remote(group, carry):
        build_tiles(remote_tiles, group, at_slot_tile, at_slot_side)
        return carry

    def build_local(group, carry):
        build_tiles(local_tiles, group, at_tile, at_side)
        return carry

    route_rows = row_pairs * HALF

    def build_route(m, carry):
        row = lax.broadcasted_iota(jnp.int32, (route_rows, LANES), 0)
        col = lax.broadcasted_iota(jnp.int32, (route_rows, LANES), 1)
        wide = lax.broadcasted_iota(jnp.int32, (1, LANES), 1) < BLOCK
        asked = jnp.where(wide, want[2 * m], want[2 * m + 1])
        target = jnp.where(asked < row_pairs, asked, jnp.where(asked == row_pairs, -row_pairs, asked - near_pairs))
        hit = row - col % HALF == target * HALF
        at = pl.ds(pl.multiple_of(m * route_rows, route_rows), route_rows)
        route[at, :] = jnp.where(hit, 1.0, 0.0).astype(BF16)
        return carry

    def show(out, u, group, blocks):
        for i in range(pair_group):
            at = pl.ds(pl.multiple_of((group * pair_group + i) * LANES, LANES), LANES)
            out[u * HALF : (u + 1) * HALF, at] = blocks[i]

    for step in range(STEPS):
        for u in range(HALVES):
            if (step, u) == (1, 0):
                lax.fori_loop(0, chunks // 4, build_local, 0)
            elif (step, u) == (1, 1):
                lax.fori_loop(chunks // 4, chunks // 2, build_local, 0)
            elif (step, u) == (2, 0):
                lax.fori_loop(0, peers, build_remote, 0)
            elif (step, u) == (2, 1):
                lax.fori_loop(0, doms // 2, build_route, 0)
                acc[chunks] = jnp.zeros((HALF, LANES), F32)
                blank = jnp.zeros((PAIRS, HALF, LANES), BF16)
                for late in range(STEPS):
                    for v in range(HALVES):
                        back_buf[late, v, pl.ds(peers * PAIRS, PAIRS)] = blank
            exchange(step, u, 0, peers).wait_recv()
            here = table[step][u]

            def turn_some(first, count):
                here[pl.ds(far_pairs + first, count)] = turn(here[pl.ds(first, count)])

            def turn_group(group, carry):
                turn_some(row_pairs + group * 2 * GROUP, 2 * GROUP)
                return carry

            whole_groups = peers * PAIRS // (2 * GROUP)
            lax.fori_loop(0, whole_groups, turn_group, 0)
            done = whole_groups * 2 * GROUP
            turn_some(row_pairs + done, peers * PAIRS - done)

            def propagate(group, carry):
                sums = []
                for i in range(GROUP):
                    r = group * GROUP + i
                    picked = [two(here, index[8 * r + 2 * q], index[8 * r + 2 * q + 1]) for q in range(4)]
                    sums.append(row_products(jnp.concatenate(picked, axis=1), r))
                sums = jnp.stack([jnp.concatenate(sums[2 * i : 2 * i + 2], axis=1) for i in range(pair_group)])
                at, later = places(group)
                rounded, teleport = near[u][at].astype(F32), teleports[at, u].astype(F32)
                state = (1.0 - TELEPORT) * ((sums + rounded) * inverse[at]) + TELEPORT * teleport
                if step + 1 < STEPS:
                    keep_state(step + 1, u, at, later, state.astype(BF16))
                else:
                    final[u, at] = state
                    show(prop_out, u, group, state)
                return carry

            lax.fori_loop(0, groups, propagate, 0)
            if step + 1 < STEPS:
                send_state(step + 1, u)

    def class_id(u):
        return my_col * share + u * HALF + lax.broadcasted_iota(jnp.int32, (HALF, LANES), 0)

    state = [final[u] for u in range(HALVES)]
    usable = [class_id(u) < classes for u in range(HALVES)]
    top = functools.reduce(
        jnp.maximum, [jnp.max(jnp.where(usable[u], state[u], FILL), axis=1) for u in range(HALVES)]
    )
    sums = functools.reduce(
        jnp.add,
        [
            jnp.sum(jnp.where(usable[u], jnp.exp(state[u] - top[:, None, :]), 0.0), axis=1)
            for u in range(HALVES)
        ],
    )
    stat_send[0] = top
    stat_send[1] = sums

    def stat_copy(j):
        return pltpu.make_async_remote_copy(
            src_ref=stat_send,
            dst_ref=stat_recv.at[j],
            send_sem=stat_sems.at[0, j],
            recv_sem=stat_sems.at[1, j],
            device_id={"col": col_at(j + 1)},
            device_id_type=MESH,
        )

    for j in range(cols - 1):
        stat_copy(j).start()
    for j in range(cols - 1):
        stat_copy(j).wait_recv()
    tops = [stat_send[0]] + [stat_recv[j, 0] for j in range(cols - 1)]
    sums = [stat_send[1]] + [stat_recv[j, 1] for j in range(cols - 1)]
    top = functools.reduce(jnp.maximum, tops)
    whole = functools.reduce(jnp.add, [s * jnp.exp(t - top) for s, t in zip(sums, tops)])
    stat_recv[0, 0] = top
    stat_recv[0, 1] = 1.0 / whole

    def send_products(late, u):
        def products_for(k):
            ready = []
            for t in range(PAIRS):
                slot = at_slot_row + CAP * k + 2 * t
                at = pl.ds(pl.multiple_of((k * PAIRS + t) * LANES, LANES), LANES)
                left = two(near[u], index[slot], index[slot + 1])
                ready.append(jnp.dot(left, remote_tiles[at, :], preferred_element_type=F32))
            return jnp.stack(ready).astype(BF16)

        send_all(STEPS + late, u, products_for)

    for u in range(HALVES):

        def cotangent(group, carry):
            at, later = places(group)
            rows = pl.ds(group * pair_group, pair_group)
            expo = jnp.exp(final[u, at] - stat_recv[0, 0, rows, :][:, None, :])
            probs = expo * stat_recv[0, 1, rows, :][:, None, :]
            coded = code[at]
            onehot = jnp.where(class_id(u) == coded % 256, 1.0, 0.0)
            weight = (coded // 256).astype(F32)
            gradient = jnp.where(usable[u], weight * (probs - onehot), 0.0)
            grad[u, at] = TELEPORT * gradient
            keep_state(None, u, at, later, (inverse[at] * gradient).astype(BF16))
            return carry

        lax.fori_loop(0, groups, cotangent, 0, unroll=True)
        send_products(0, u)

    nothing = jnp.zeros((HALF, LANES), BF16)
    half_of = jnp.where(low, 0, 1)

    for late in range(STEPS):
        for u in range(HALVES):

            def local_chunks(group, running):
                terms = []
                for i in range(GROUP):
                    m = group * GROUP + i
                    left = two(near[u], index[at_row + 2 * m], index[at_row + 2 * m + 1])
                    weights = local_tiles[pl.ds(pl.multiple_of(m * LANES, LANES), LANES), :]
                    terms.append(jnp.dot(left, weights, preferred_element_type=F32))
                sums = []
                for i in range(GROUP):
                    running = running * index[at_keep + group * GROUP + i].astype(F32) + terms[i]
                    sums.append(running)
                acc[pl.ds(group * GROUP, GROUP)] = jnp.stack(sums)
                return running

            lax.fori_loop(0, chunks // GROUP, local_chunks, jnp.zeros((HALF, LANES), F32))

            def local_sum(group, carry):
                picked = [acc[index[at_last + group * GROUP + i]] for i in range(GROUP)]
                come_in[pl.ds(group * pair_group, pair_group)] = jnp.stack(
                    [picked[2 * i] + picked[2 * i + 1] for i in range(pair_group)]
                )
                return carry

            lax.fori_loop(0, groups, local_sum, 0)
            exchange(STEPS + late, u, 0, peers).wait_recv()

            def arrive(m, carry):
                first = [pl.multiple_of((2 * m + i) * route_rows, route_rows) for i in range(2)]
                left = jnp.concatenate([route[pl.ds(f, route_rows), :] for f in first], axis=1)
                part = back_buf[late, u, pl.ds(m * 4 * PAIRS, 4 * PAIRS)]
                flipped = turn(part)
                both = jnp.where(low, part, flipped), jnp.where(low, flipped, part)
                rows = []
                for i in range(4 * CAP):
                    asked = want_s[4 * m + i // CAP, 0, HALF * (i % CAP)]
                    goal = jnp.where(asked < near_pairs, i % 2, 1 - i % 2)
                    rows.append(jnp.where(half_of == goal, both[i % 2][i // 2], nothing))
                sums = jnp.dot(left, jnp.concatenate(rows, axis=0), preferred_element_type=F32)
                come_in[...] += sums.reshape(row_pairs, HALF, LANES)
                return carry

            lax.fori_loop(0, doms // 4, arrive, 0)

            def finish(group, carry):
                at, later = places(group)
                gradient = (1.0 - TELEPORT) * (come_in[at] + near[u][at].astype(F32))
                if late < STEPS - 1:
                    grad[u, at] += TELEPORT * gradient
                    keep_state(None, u, at, later, (inverse[at] * gradient).astype(BF16))
                else:
                    show(grad_out, u, group, grad[u, at] + gradient)
                return carry

            lax.fori_loop(0, groups, finish, 0)
            if late < STEPS - 1:
                send_products(late + 1, u)

    all_requests().wait_send()
    for j in range(cols - 1):
        head_copy(j).wait_send()
        stat_copy(j).wait_send()
    for step in range(2 * STEPS):
        for u in range(HALVES):
            exchange(step, u, 0, peers).wait_send()


def body(features, w_hidden, w_out, block_values, block_slot, requested, labels, train_mask):
    doms, cols = lax.axis_size("dom"), lax.axis_size("col")
    nodes = labels.shape[0]
    row_blocks = nodes // BLOCK
    row_pairs = row_blocks // 2
    share = w_out.shape[1] // cols
    entries = block_slot.shape[0]
    index, chunks = index_tables(block_slot, doms, row_blocks)
    side = jnp.arange(CAP, dtype=jnp.int32) % 2
    asked = requested // 2 + jnp.where(requested % 2 == side, 0, row_pairs + 1)
    asked = jnp.where(requested < 0, row_pairs, asked)
    request = jnp.broadcast_to(asked.reshape(doms, 1, 1, CAP, 1), (doms, 1, 2, CAP, HALF)).reshape(doms, 1, LANES)
    code = (labels + 256 * train_mask).reshape(row_pairs, 1, LANES)
    peers = doms - 1
    far_pairs = row_pairs + peers * PAIRS
    rows = BLOCK * BLOCK // LANES
    mine = features.shape[0] // LANES
    vmem, dma = pltpu.VMEM, pltpu.SemaphoreType.DMA
    block = (HALF, LANES)
    in_vmem = pl.BlockSpec(memory_space=pltpu.VMEM)
    anywhere = pl.BlockSpec(memory_space=pl.ANY)
    return pl.pallas_call(
        functools.partial(kernel, doms, cols, NCLASS, chunks),
        out_shape=[jax.ShapeDtypeStruct((share, nodes), F32)] * 2,
        in_specs=[pl.BlockSpec(memory_space=pltpu.SMEM)] + [anywhere] * 4 + [in_vmem] * 2,
        out_specs=[in_vmem] * 2,
        scratch_shapes=[
            vmem(features.shape, BF16),
            vmem(w_hidden.shape, BF16),
            vmem(w_out.shape, BF16),
            vmem((entries, BLOCK * BLOCK), BF16),
            vmem((SPREAD * rows, LANES), F32),
            vmem((SPREAD * rows, LANES), F32),
            vmem((entries // 2, BLOCK, LANES), BF16),
            vmem((cols * mine, HALVES, *block), BF16),
            vmem((2, row_pairs, LANES), F32),
            vmem((cols - 1, 2, row_pairs, LANES), F32),
            vmem((doms, 1, LANES), jnp.int32),
            pltpu.SMEM((doms, 1, LANES), jnp.int32),
            vmem((row_pairs, HALVES, *block), BF16),
            *[vmem((2 * far_pairs, *block), BF16) for _ in range(STEPS * HALVES)],
            *[vmem((2 * (row_pairs + 1), *block), BF16) for _ in range(HALVES)],
            vmem((row_pairs, *block), F32),
            vmem((HALVES, row_pairs, *block), F32),
            vmem((HALVES, row_pairs, *block), F32),
            vmem((chunks + 1, *block), F32),
            vmem((row_pairs, *block), F32),
            vmem((peers * CAP * BLOCK, LANES), BF16),
            vmem((2 * chunks * BLOCK, LANES), BF16),
            vmem((doms // 2 * row_pairs * HALF, LANES), BF16),
            vmem((2 * STEPS, HALVES, peers * PAIRS, *block), BF16),
            vmem((STEPS, HALVES, doms * PAIRS, *block), BF16),
            dma((2, cols - 1)),
            dma((2, cols - 1)),
            dma((2,)),
            dma((5,)),
            dma((2 * STEPS, HALVES)),
            dma((2 * STEPS, HALVES)),
        ],
        compiler_params=pltpu.CompilerParams(
            collective_id=0, has_side_effects=True, vmem_limit_bytes=48 * 2**20
        ),
    )(index, features, w_hidden, w_out, block_values, request, code)


def solution(mesh):
    return jax.shard_map(
        body,
        mesh=mesh,
        in_specs=(
            P(("dom", "col"), None),
            P(),
            P(),
            P("dom", None),
            P("dom"),
            P("dom", None, None),
            P("dom"),
            P("dom"),
        ),
        out_specs=(P("col", "dom"), P("col", "dom")),
        check_vma=False,
    )
```
